256 devices in a mesh: dp: 8 (over x, core), expert: 32 (over y, z).
Axes of the slice: x: 4, y: 4, z: 8, core: 2. Of those that a mesh axis runs over, the one named last changes fastest.
Arguments:
- tokens: bfloat16 [49152, 1024], P(('dp', 'expert')), may hold values from -6 to 6
- route_ids: int32 [49152, 4], P(('dp', 'expert')), may hold values from 0 to 31, all different within a row; in each aligned block of 192 rows (0 to 191, 192 to 383, ...) at most 36 rows name the same one
- gate_weight: float32 [49152, 4], P(('dp', 'expert')), may hold values from 0.25 to 1
- old_owner: int32 [32], replicated, may hold values from 0 to 31, as said below
- new_owner: int32 [32], replicated, may hold values from 0 to 31, as said below
- weights: bfloat16 [32, 3, 1024, 1024], P('expert', None, None, 'dp'), may hold values from -0.1875 to 0.1875
- first_moment: float32 [32, 3, 1024, 1024], P('expert', None, None, 'dp'), may hold values from -6 to 6
- second_moment: float32 [32, 3, 1024, 1024], P('expert', None, None, 'dp'), may hold values from 0.01 to 4
Outputs:
- layer_output: bfloat16 [49152, 1024], P(('dp', 'expert'))
- new_weights: bfloat16 [32, 3, 1024, 1024], P('expert', None, None, 'dp')
- new_first_moment: float32 [32, 3, 1024, 1024], P('expert', None, None, 'dp')
- new_second_moment: float32 [32, 3, 1024, 1024], P('expert', None, None, 'dp')
The draws below stay inside these ranges and needn't reach their ends.
Inputs may be any that keep to these rules, and one draw needn't show every extreme that they name: `old_owner`: A permutation of the slots. `new_owner`: A permutation of the slots that differs from old_owner in exactly 5 experts. `route_ids`: the 4 experts of a row differ. In the 192 rows of one device no expert is named more than 36 times, a bound that some block reaches.
All inputs are finite; a program needn't handle non-finite values.
Results may differ from the reference program's by a relative error of at most 0.0058.
Values may be sent and summed in bfloat16 or wider, within the bound.
A program may use at most 128 MiB of HBM per device.

```python
import math
import jax
import jax.numpy as jnp
import numpy as np
from jax import lax

D = 1024
H = 1024
TOP = 4
TOK_DEV = 192
EXPERTS = 32
CAP = 36
MOVES = 5
TOKENS = 49152
N_DP = 8
N_EXPERT = 32


def owner_plan(key):
    base = jax.random.fold_in(key, 7)
    first_key, second_key = jax.random.split(base)
    before = jax.random.permutation(first_key, EXPERTS).astype(jnp.int32)
    moving = jax.random.permutation(second_key, EXPERTS)[:MOVES].astype(jnp.int32)
    after = before.at[moving].set(before[jnp.roll(moving, 1)])
    return (before, after)


def draw_old_owner(key, part):
    return owner_plan(key)[0]


def draw_new_owner(key, part):
    return owner_plan(key)[1]


def shard_levels(stream_key, dims, cuts, least, high):
    factor_of = 1.0
    for dim, shards_of in cuts:
        draws = jax.random.uniform(jax.random.fold_in(jax.random.fold_in(stream_key, 6), dim), (shards_of,), jnp.float32, least / len(cuts), high / len(cuts))
        factor_of = factor_of * jnp.repeat(jnp.exp(draws), dims[dim] // shards_of).reshape((-1,) + (1,) * (len(dims) - 1 - dim))
    return factor_of


def assign_block(stream_key, own, number, rows, number_of, top, bound, slope):
    ranking = jax.random.permutation(stream_key, number_of)
    crowded, usual = shares(number_of, rows * top, bound, slope, True), shares(number_of, rows * top, bound, slope, False)
    places = jnp.arange(number_of)

    def named(lengths, offset_by):
        used = int((lengths > 0).sum())
        fixed = max(1, used // 4)
        moved = fixed + (places - fixed + offset_by * (used - fixed)) % max(1, number_of - fixed)
        return jnp.zeros((number_of,), jnp.int32).at[ranking[jnp.where(places < fixed, places, moved)]].set(jnp.asarray(lengths, jnp.int32))

    lengths = jnp.where(number % 4 == 0, named(crowded, number // 4), named(usual, number - number // 4 - 1))
    mixed = jax.random.permutation(jax.random.fold_in(own, 3), number_of)
    giver, taker = mixed[0:number_of // 2 * 2:2], mixed[1:number_of // 2 * 2:2]
    room = jnp.minimum(lengths[giver] - 1, bound - lengths[taker]) // 2
    room = jnp.where((giver == ranking[0]) | (taker == ranking[0]) | (lengths[taker] == 0), 0, jnp.maximum(room, 0))
    moved = jax.random.randint(jax.random.fold_in(own, 4), (number_of // 2,), 0, 1 << 20) % (room + 1)
    lengths = lengths.at[giver].add(-moved).at[taker].add(moved)
    items = jnp.searchsorted(jnp.cumsum(lengths), jnp.arange(rows * top), side="right").astype(jnp.int32)
    table = items.reshape(top, rows).T
    table = table[jax.random.permutation(jax.random.fold_in(own, 1), rows)]
    offset_by = jax.random.randint(jax.random.fold_in(own, 2), (rows, 1), 0, top)
    return jnp.take_along_axis(table, (jnp.arange(top)[None, :] + offset_by) % top, axis=1)


def shares(count, total, bound, slope, full):
    portions = [(1 << 20) // math.isqrt(grade ** slope) + 1 for grade in range(1, count + 1)]
    largest = bound if full else min(bound, max(-(-total // count), total * portions[0] // sum(portions)))
    least = 1 if total - largest >= count - 1 else 0
    holding, surplus = [largest] + [least] * (count - 1), total - largest - least * (count - 1)
    while surplus > 0:
        free = [i for i in range(1, count) if holding[i] < largest] or [i for i in range(1, count) if holding[i] < bound]
        whole, remaining = sum([portions[i] for i in free]), surplus
        for i in free:
            more = min(bound - holding[i], max(1, remaining * portions[i] // whole), surplus)
            holding[i] = holding[i] + more
            surplus = surplus - more
    return np.array(holding)


def noise(rng, extent, deviation, bound, shards=(), held_as=jnp.bfloat16):
    loudness = shard_levels(rng, extent, shards, -0.22, 0.18) if shards else 1.0
    entries = jax.random.normal(rng, extent, jnp.float32) * deviation * loudness
    return jnp.minimum(jnp.maximum(entries, -bound), bound).astype(held_as)


def setup_inputs(seed: int = 0) -> dict:
    splits = jax.random.split(jax.random.key(seed), 9)
    tokens = noise(splits[0], (TOKENS, D), 1.0, 6.0, ((0, 256),))
    route_ids_keys = jax.random.split(jax.random.fold_in(splits[1], 1), TOKENS // TOK_DEV)
    route_ids_turns = jax.random.permutation(jax.random.fold_in(splits[1], 3), TOKENS // TOK_DEV)
    route_ids = jax.vmap(lambda own, number: assign_block(jax.random.fold_in(splits[1], 2), own, number, TOK_DEV, EXPERTS, TOP, CAP, 2))(route_ids_keys, route_ids_turns).reshape((TOKENS, TOP))
    gate_weight = jnp.clip(0.25 + 0.75 * jax.random.uniform(splits[2], (TOKENS, TOP), jnp.float32) ** shard_levels(splits[2], (TOKENS, TOP), ((0, 256),), -0.2, 0.2), 0.25, 1.0)
    old_owner = draw_old_owner(jax.random.fold_in(splits[8], 71), 0)
    new_owner = draw_new_owner(jax.random.fold_in(splits[8], 71), 0)
    weights = noise(splits[5], (EXPERTS, 3, D, H), D ** -0.5, 0.1875, ((0, 32), (3, 8)))
    first_moment = noise(splits[6], (EXPERTS, 3, D, H), 1.0, 6.0, ((0, 32), (3, 8)), jnp.float32)
    second_moment = jnp.clip(jnp.exp(math.log(4.0) - 5.9914646 * jax.random.uniform(splits[7], (EXPERTS, 3, D, H), jnp.float32) ** shard_levels(splits[7], (EXPERTS, 3, D, H), ((0, 32), (3, 8)), -0.2, 0.2)), 0.01, 4.0)
    return {"tokens": tokens, "route_ids": route_ids, "gate_weight": gate_weight, "old_owner": old_owner, "new_owner": new_owner, "weights": weights, "first_moment": first_moment, "second_moment": second_moment}


def reference(tokens, route_ids, gate_weight, old_owner, new_owner, weights, first_moment, second_moment):
    source_slot = jnp.zeros((EXPERTS,), jnp.int32).at[new_owner].set(old_owner)
    new_weights = jnp.take(weights, source_slot, axis=0)
    new_first = jnp.take(first_moment, source_slot, axis=0)
    new_second = jnp.take(second_moment, source_slot, axis=0)
    expert_ids = route_ids.reshape(-1)
    count_all = expert_ids.shape[0]
    labels = jnp.arange(EXPERTS, dtype=jnp.int32)
    matches = (expert_ids[:, None] == labels[None, :]).astype(jnp.int32)
    position = jnp.sum((jnp.cumsum(matches, axis=0) - 1) * matches, axis=1).astype(jnp.int32)
    limit = CAP * N_DP * N_EXPERT
    token_index = (jnp.arange(count_all, dtype=jnp.int32) // TOP).astype(jnp.int32)
    table = jnp.zeros((EXPERTS, limit), jnp.int32).at[expert_ids, position].set(token_index)
    by_expert = jnp.take(weights, old_owner, axis=0)

    def run_expert(item):
        row_index, matrices = item
        chosen = jnp.take(tokens, row_index, axis=0)
        gate_part = jnp.dot(chosen, matrices[0], preferred_element_type=jnp.float32)
        up_part = jnp.dot(chosen, matrices[1], preferred_element_type=jnp.float32)
        hidden = (jax.nn.silu(gate_part) * up_part).astype(jnp.bfloat16)
        return jnp.dot(hidden, matrices[2].T, preferred_element_type=jnp.float32).astype(jnp.bfloat16)

    results = lax.map(run_expert, (table, by_expert))
    picked = results[expert_ids, position].astype(jnp.float32).reshape(TOKENS, TOP, D)
    layer_output = jnp.sum(picked * gate_weight[:, :, None], axis=1).astype(jnp.bfloat16)
    return (layer_output, new_weights, new_first, new_second)
```

```python
import functools

import jax
import jax.numpy as jnp
from jax import lax
from jax.experimental import pallas as pl
from jax.experimental.pallas import tpu as pltpu
from jax.sharding import PartitionSpec as P

MESH = pl.DeviceIdType.MESH
F32 = jnp.float32
BF16 = jnp.bfloat16
META = 16


class Plan:
    def __init__(self, n_dp, n_y, n_z, tok, cap, d, hs):
        self.nx, self.ny, self.nz = n_dp // 2, n_y, n_z
        self.tok, self.cap, self.d, self.hs = tok, cap, d, hs
        self.half = n_z // 2
        order = [0]
        for s in range(1, self.half):
            order += [s, n_z - s]
        order += [self.half]
        self.groups = (order[: self.half], order[self.half :])
        self.rows = self.half * cap
        self.yorder = [0, 1, 3, 2] if n_y == 4 else list(range(n_y))
        cut = tok // 2
        self.agcut = ((0, cut), (cut, tok + META - cut))
        self.rscut = ((0, cut), (cut, tok - cut))
        self.ag = [
            (way, part, s)
            for s in range(1, self.half + 1)
            for way in (0, 1)
            for part in (0, 1)
            if s < self.half or way == part
        ]
        self.rs = [
            (way, part, dist)
            for dist in range(self.half, 0, -1)
            for way in (0, 1)
            for part in (0, 1)
            if dist < self.half or way == part
        ]


def moe_kernel(
    p,
    tokx,
    wts,
    out,
    tokb,
    sendb,
    recvd,
    wall,
    res,
    rret,
    part,
    rsin,
    rsout,
    acc,
    prow,
    pcol,
    lsem,
    ags,
    agr,
    xs,
    xr,
    ds,
    dr,
    es,
    er,
    rss,
    rsr,
):
    ny, nz, nx = p.ny, p.nz, p.nx
    dp = lax.axis_index("dp")
    ex = lax.axis_index("expert")
    x, core = dp // 2, dp % 2
    y, z = ex // nz, ex % nz
    right = (dp, y * nz + (z + 1) % nz)
    left = (dp, y * nz + (z + nz - 1) % nz)
    above = [None] + [(dp, ((y + j) % ny) * nz + z) for j in range(1, ny)]
    twin = (x * 2 + 1 - core, ex)
    xright = (((x + 1) % nx) * 2 + core, ex)
    xleft = (((x + nx - 1) % nx) * 2 + core, ex)

    barrier = pltpu.get_barrier_semaphore()
    peers = [right, left, twin] + above[1:] + ([xright, xleft] if nx > 1 else [])
    for peer in peers:
        pl.semaphore_signal(barrier, inc=1, device_id=peer, device_id_type=MESH)
    pl.semaphore_wait(barrier, len(peers))

    def remote(src, dst, send, recv, to):
        return pltpu.make_async_remote_copy(
            src_ref=src, dst_ref=dst, send_sem=send, recv_sem=recv, device_id=to, device_id_type=MESH
        )

    started = []

    def go(copy):
        copy.start()
        started.append(copy)
        return copy

    def tok(r):
        return tokx if r == 0 else tokb.at[r - 1]

    def ag_copy(way, half, s):
        src = (nz - (s - 1)) % nz if way == 0 else s - 1
        dst = nz - s if way == 0 else s
        first, size = p.agcut[half]
        n = p.ag.index((way, half, s))
        return remote(
            tok(src).at[pl.ds(first, size)],
            tok(dst).at[pl.ds(first, size)],
            ags.at[n],
            agr.at[n],
            right if way == 0 else left,
        )

    agc = {}

    def ag_start(s):
        for way, half, step in p.ag:
            if step == s:
                if s > 1:
                    agc[way, half, s - 1].wait_recv()
                agc[way, half, s] = go(ag_copy(way, half, s))
        if s == p.half:
            for way in (0, 1):
                if s > 1:
                    agc[way, 1 - way, s - 1].wait_recv()

    ag_start(1)

    hd = p.d // 2
    keep = pltpu.make_async_copy(wts, wall.at[0, 0], lsem.at[0])
    keep.start()
    xc = [go(remote(wts, wall.at[0, 1], xs.at[0], xr.at[0], twin))]
    if nx > 1:
        xc.append(go(remote(wts, wall.at[3, 0], xs.at[1], xr.at[1], xright)))
        xc.append(go(remote(wts, wall.at[1, 0], xs.at[2], xr.at[2], xleft)))

    def x_second():
        if nx > 1:
            lo, hi = pl.ds(0, hd), pl.ds(hd, hd)
            xc[1].wait_recv()
            xc.append(go(remote(wall.at[3, 0, :, lo], wall.at[2, 0, :, lo], xs.at[3], xr.at[3], xright)))
            xc.append(go(remote(wall.at[3, 0], wall.at[3, 1], xs.at[4], xr.at[4], twin)))
            xc[2].wait_recv()
            xc.append(go(remote(wall.at[1, 0, :, hi], wall.at[2, 0, :, hi], xs.at[5], xr.at[5], xleft)))
            xc.append(go(remote(wall.at[1, 0], wall.at[1, 1], xs.at[6], xr.at[6], twin)))

    def x_third():
        if nx > 1:
            xc[3].wait_recv()
            xc[5].wait_recv()
            xc.append(go(remote(wall.at[2, 0], wall.at[2, 1], xs.at[7], xr.at[7], twin)))

    def x_ready():
        keep.wait()
        xc[0].wait_recv()
        if nx > 1:
            for n in (4, 6, 7):
                xc[n].wait_recv()

    tok_n = p.tok
    ta = lax.broadcasted_iota(jnp.int32, (tok_n, tok_n), 0)
    tb = lax.broadcasted_iota(jnp.int32, (tok_n, tok_n), 1)
    before = (ta < tb).astype(F32).astype(BF16)
    after = (tb < ta).astype(F32).astype(BF16)
    same = (ta == tb).astype(F32).astype(BF16)
    jrow = lax.broadcasted_iota(jnp.int32, (8, 1), 0)
    yrow = jnp.where(jrow + y >= ny, jrow + y - ny, jrow + y)
    column = jnp.where(jrow < ny, yrow * nz + z, -5).astype(F32)
    nt = (((1,), (1,)), ((), ()))

    def places(r):
        m = tok(r)[pl.ds(tok_n, META), pl.ds(0, tok_n)].astype(F32)
        named = jnp.zeros((8, tok_n), F32)
        ghi = jnp.zeros((8, tok_n), F32)
        glo = jnp.zeros((8, tok_n), F32)
        for k in range(4):
            hit = m[k : k + 1] == column
            named = named + jnp.where(hit, 1.0, 0.0)
            ghi = ghi + jnp.where(hit, m[4 + k : 5 + k], 0.0)
            glo = glo + jnp.where(hit, m[8 + k : 9 + k], 0.0)
        nb = named.astype(BF16)
        rank = jnp.dot(nb, before, preferred_element_type=F32)
        prow[r] = jnp.where(named > 0.5, rank, -4096.0)
        rank_c = lax.dot_general(after, nb, nt, preferred_element_type=F32)
        named_c = lax.dot_general(same, nb, nt, preferred_element_type=F32)
        gate_c = lax.dot_general(same, ghi.astype(BF16), nt, preferred_element_type=F32) + lax.dot_general(
            same, glo.astype(BF16), nt, preferred_element_type=F32
        )
        pcol[r, :, pl.ds(0, 8)] = jnp.where(named_c > 0.5, rank_c, -4096.0)
        pcol[r, :, pl.ds(8, 8)] = gate_c

    crow = lax.broadcasted_iota(jnp.int32, (p.rows, tok_n), 0).astype(F32)
    dc = {}
    nslot = 2 * ny

    def dispatch(h):
        for j in list(range(1, ny)) + [0]:
            total = jnp.zeros((p.rows, p.d), F32)
            for i, r in enumerate(p.groups[h]):
                pick = jnp.where(prow[r, j : j + 1, :] + float(i * p.cap) == crow, 1.0, 0.0).astype(BF16)
                total = total + jnp.dot(pick, tok(r)[pl.ds(0, tok_n)], preferred_element_type=F32)
            total = total.astype(BF16)
            if j == 0:
                recvd[pl.ds(h * ny * p.rows, p.rows)] = total
            else:
                n = h * (ny - 1) + j - 1
                sendb[n] = total
                pos = p.yorder.index((ny - j) % ny)
                dc[h, pos] = go(
                    remote(
                        sendb.at[n], recvd.at[pl.ds((h * ny + pos) * p.rows, p.rows)], ds.at[n], dr.at[n], above[j]
                    )
                )

    ec = {}

    def expert(h, first, count):
        base = (h * ny + first) * p.rows
        size = count * p.rows
        for pos in range(first, first + count):
            if pos > 0:
                dc[h, pos].wait_recv()

        def chunk(c, carry):
            xin = recvd[pl.ds(base, size)]
            wg = jnp.concatenate([wall[c, 0, 0], wall[c, 1, 0]], axis=1)
            wu = jnp.concatenate([wall[c, 0, 1], wall[c, 1, 1]], axis=1)
            wd = jnp.concatenate([wall[c, 0, 2], wall[c, 1, 2]], axis=1)
            g = jnp.dot(xin, wg, preferred_element_type=F32)
            u = jnp.dot(xin, wu, preferred_element_type=F32)
            hid = (g / (1.0 + jnp.exp(-g)) * u).astype(BF16)
            add = lax.dot_general(hid, wd, nt, preferred_element_type=F32)
            acc[pl.ds(0, size)] = acc[pl.ds(0, size)] + add
            return carry

        acc[pl.ds(0, size)] = jnp.zeros((size, p.d), F32)
        lax.fori_loop(0, nx, chunk, 0)
        res[pl.ds(base, size)] = acc[pl.ds(0, size)].astype(BF16)
        for pos in range(first, first + count):
            if pos > 0:
                o = p.yorder[pos]
                j = ny - o
                n = h * (ny - 1) + j - 1
                ec[h, j] = go(
                    remote(
                        res.at[pl.ds((h * ny + pos) * p.rows, p.rows)], rret.at[n], es.at[n], er.at[n], above[o]
                    )
                )

    ccol = lax.broadcasted_iota(jnp.int32, (tok_n, p.rows), 1).astype(F32)

    def combine(r):
        h = 0 if r in p.groups[0] else 1
        i = p.groups[h].index(r)
        total = jnp.zeros((tok_n, p.d), F32)
        for j in range(ny):
            pick = jnp.where(pcol[r, :, j : j + 1] + float(i * p.cap) == ccol, 1.0, 0.0).astype(BF16)
            rows = res[pl.ds(h * ny * p.rows, p.rows)] if j == 0 else rret[h * (ny - 1) + j - 1]
            total = total + pcol[r, :, 8 + j : 9 + j] * jnp.dot(pick, rows, preferred_element_type=F32)
        part[r] = total

    places(0)
    for s in range(2, p.half):
        ag_start(s)
        places(s - 1)
        places(nz - s + 1)
    ag_start(p.half)
    places(p.half - 1)
    places(nz - p.half + 1)
    dispatch(0)
    x_second()
    for way in (0, 1):
        agc[way, way, p.half].wait_recv()
    places(p.half)
    dispatch(1)
    x_third()
    x_ready()
    for h in (0, 1):
        for first in range(0, ny, 2):
            expert(h, first, min(2, ny - first))
    for h in (0, 1):
        for j in range(1, ny):
            ec[h, j].wait_recv()
        for r in sorted(p.groups[h], key=lambda r: -min(r, nz - r)):
            combine(r)

    rc = {}
    for way, half, dist in p.rs:
        n = p.rs.index((way, half, dist))
        first, size = p.rscut[half]
        off = dist if way == 0 else nz - dist
        total = part[off, pl.ds(first, size)]
        if (way, half, dist + 1) in rc:
            rc[way, half, dist + 1].wait_recv()
            total = total + rsin[p.rs.index((way, half, dist + 1)), pl.ds(0, size)].astype(F32)
        rsout[n, pl.ds(0, size)] = total.astype(BF16)
        rc[way, half, dist] = go(
            remote(
                rsout.at[n, pl.ds(0, size)],
                rsin.at[n, pl.ds(0, size)],
                rss.at[n],
                rsr.at[n],
                right if way == 0 else left,
            )
        )
    for half in (0, 1):
        first, size = p.rscut[half]
        total = part[0, pl.ds(first, size)]
        for way in (0, 1):
            rc[way, half, 1].wait_recv()
            total = total + rsin[p.rs.index((way, half, 1)), pl.ds(0, size)].astype(F32)
        out[pl.ds(first, size)] = total.astype(BF16)
    for copy in started:
        copy.wait_send()


def moe(p, tokx, weights):
    ny, nz, nx = p.ny, p.nz, p.nx
    dma = pltpu.SemaphoreType.DMA
    flat = weights
    return pl.pallas_call(
        functools.partial(moe_kernel, p),
        out_shape=jax.ShapeDtypeStruct((p.tok, p.d), BF16),
        in_specs=[pl.BlockSpec(memory_space=pltpu.VMEM), pl.BlockSpec(memory_space=pl.ANY)],
        out_specs=pl.BlockSpec(memory_space=pltpu.VMEM),
        scratch_shapes=[
            pltpu.VMEM((nz - 1, p.tok + META, p.d), BF16),
            pltpu.VMEM((2 * (ny - 1), p.rows, p.d), BF16),
            pltpu.VMEM((2 * ny * p.rows, p.d), BF16),
            pltpu.VMEM((nx, 2, 3, p.d, p.hs), BF16),
            pltpu.VMEM((2 * ny * p.rows, p.d), BF16),
            pltpu.VMEM((2 * (ny - 1), p.rows, p.d), BF16),
            pltpu.VMEM((nz, p.tok, p.d), F32),
            pltpu.VMEM((len(p.rs), p.tok // 2, p.d), BF16),
            pltpu.VMEM((len(p.rs), p.tok // 2, p.d), BF16),
            pltpu.VMEM((2 * p.rows, p.d), F32),
            pltpu.VMEM((nz, 8, p.tok), F32),
            pltpu.VMEM((nz, p.tok, 128), F32),
            dma((1,)),
            dma((len(p.ag),)),
            dma((len(p.ag),)),
            dma((8,)),
            dma((8,)),
            dma((2 * (ny - 1),)),
            dma((2 * (ny - 1),)),
            dma((2 * (ny - 1),)),
            dma((2 * (ny - 1),)),
            dma((len(p.rs),)),
            dma((len(p.rs),)),
        ],
        compiler_params=pltpu.CompilerParams(
            collective_id=0, has_side_effects=True, vmem_limit_bytes=60 * 1024 * 1024
        ),
        name="moe",
    )(tokx, flat)


def reorder(blocks, source_slot):
    n, rows, lanes = blocks.shape

    def copy(order, src, dst):
        dst[...] = src[...]

    return pl.pallas_call(
        copy,
        grid_spec=pltpu.PrefetchScalarGridSpec(
            num_scalar_prefetch=1,
            grid=(n,),
            in_specs=[pl.BlockSpec((1, rows, lanes), lambda s, order: (order[s], 0, 0))],
            out_specs=pl.BlockSpec((1, rows, lanes), lambda s, order: (s, 0, 0)),
        ),
        out_shape=jax.ShapeDtypeStruct(blocks.shape, blocks.dtype),
        name="reorder",
    )(source_slot, blocks)


def moves(weights, first_moment, second_moment, source_slot):
    n = lax.axis_size("expert")
    block = jnp.concatenate([weights, first_moment.astype(BF16), second_moment.astype(BF16)], axis=1)
    shape = block.shape
    block = block.reshape(n, -1, 128)
    spread = lax.all_to_all(block, "expert", split_axis=0, concat_axis=0, tiled=True)
    ordered = reorder(spread, source_slot)
    back = lax.all_to_all(ordered, "expert", split_axis=0, concat_axis=0, tiled=True).reshape(shape)
    me = lax.axis_index("expert")
    stays = source_slot[me] == me
    return (
        jnp.where(stays, weights, back[:, 0:3]),
        jnp.where(stays, first_moment, back[:, 3:6].astype(F32)),
        jnp.where(stays, second_moment, back[:, 6:9].astype(F32)),
    )


def per_device(n_y, tokens, route_ids, gate_weight, old_owner, new_owner, weights, first_moment, second_moment):
    n = lax.axis_size("expert")
    tok, d = tokens.shape
    p = Plan(lax.axis_size("dp"), n_y, n // n_y, tok, 3 * tok * route_ids.shape[1] // (2 * n), d, weights.shape[3])
    labels = jnp.arange(n, dtype=jnp.int32)
    source_slot = jnp.sum(jnp.where(new_owner[None, :] == labels[:, None], old_owner[None, :], 0), axis=1)
    slots = jnp.sum(jnp.where(route_ids[:, :, None] == labels, old_owner, 0), axis=2)
    high = lax.reduce_precision(gate_weight, 8, 7)
    meta = jnp.concatenate([slots.astype(F32), high, gate_weight - high, jnp.full((tok, META - 12), -1.0, F32)], axis=1)
    meta = jnp.pad(meta.T.astype(BF16), ((0, 0), (0, d - tok)))
    tokx = jnp.concatenate([tokens, meta], axis=0)
    layer_output = moe(p, tokx, weights[0])
    return (layer_output, *moves(weights, first_moment, second_moment, source_slot))


def solution(mesh):
    experts = mesh.shape["expert"]
    n_y = 4 if experts == 32 else 2
    placed = (
        P(("dp", "expert"), None),
        P(("dp", "expert"), None),
        P(("dp", "expert"), None),
        P(),
        P(),
        P("expert", None, None, "dp"),
        P("expert", None, None, "dp"),
        P("expert", None, None, "dp"),
    )
    return jax.shard_map(
        functools.partial(per_device, n_y),
        mesh=mesh,
        in_specs=placed,
        out_specs=(
            P(("dp", "expert"), None),
            P("expert", None, None, "dp"),
            P("expert", None, None, "dp"),
            P("expert", None, None, "dp"),
        ),
        check_vma=False,
    )
```

```python
import functools

import jax
import jax.numpy as jnp
from jax import lax
from jax.experimental import pallas as pl
from jax.experimental.pallas import tpu as pltpu
from jax.sharding import PartitionSpec as P

MESH = pl.DeviceIdType.MESH
F32 = jnp.float32
BF16 = jnp.bfloat16
META = 16


class Plan:
    def __init__(self, n_dp, n_y, n_z, tok, cap, d, hs):
        self.nx, self.ny, self.nz = n_dp // 2, n_y, n_z
        self.tok, self.cap, self.d, self.hs = tok, cap, d, hs
        self.half = n_z // 2
        order = [0]
        for s in range(1, self.half):
            order += [s, n_z - s]
        order += [self.half]
        self.groups = (order[: self.half], order[self.half :])
        self.rows = self.half * cap
        self.yorder = [0, 1, 3, 2] if n_y == 4 else list(range(n_y))
        self.chunks = 8
        self.steps = self.chunks + self.half - 1
        self.piece = 9 * d // n_y
        self.chunk = self.piece // self.chunks
        cut = tok // 2
        self.agcut = ((0, cut), (cut, tok + META - cut))
        self.rscut = ((0, cut), (cut, tok - cut))
        self.ag = [
            (way, part, s)
            for s in range(1, self.half + 1)
            for way in (0, 1)
            for part in (0, 1)
            if s < self.half or way == part
        ]
        self.rs = [
            (way, part, dist)
            for dist in range(self.half, 0, -1)
            for way in (0, 1)
            for part in (0, 1)
            if dist < self.half or way == part
        ]


def moe_kernel(
    p,
    tokx,
    wts,
    block,
    ctl,
    out,
    moved,
    tokb,
    sendb,
    recvd,
    wall,
    res,
    rret,
    part,
    rsin,
    rsout,
    acc,
    prow,
    pcol,
    spread,
    cin,
    cout,
    fin,
    lsem,
    ags,
    agr,
    xs,
    xr,
    ds,
    dr,
    es,
    er,
    rss,
    rsr,
    ss,
    sr,
    cs,
    cr,
    fs,
    fr,
):
    ny, nz, nx = p.ny, p.nz, p.nx
    dp = lax.axis_index("dp")
    ex = lax.axis_index("expert")
    x, core = dp // 2, dp % 2
    y, z = ex // nz, ex % nz
    right = (dp, y * nz + (z + 1) % nz)
    left = (dp, y * nz + (z + nz - 1) % nz)
    above = [None] + [(dp, ((y + j) % ny) * nz + z) for j in range(1, ny)]
    twin = (x * 2 + 1 - core, ex)
    xright = (((x + 1) % nx) * 2 + core, ex)
    xleft = (((x + nx - 1) % nx) * 2 + core, ex)

    barrier = pltpu.get_barrier_semaphore()
    peers = [right, left, twin] + above[1:] + ([xright, xleft] if nx > 1 else [])
    for peer in peers:
        pl.semaphore_signal(barrier, inc=1, device_id=peer, device_id_type=MESH)
    pl.semaphore_wait(barrier, len(peers))

    def remote(src, dst, send, recv, to):
        return pltpu.make_async_remote_copy(
            src_ref=src, dst_ref=dst, send_sem=send, recv_sem=recv, device_id=to, device_id_type=MESH
        )

    started = []

    def go(copy):
        copy.start()
        started.append(copy)
        return copy

    def tok(r):
        return tokx if r == 0 else tokb.at[r - 1]

    def ag_copy(way, half, s):
        src = (nz - (s - 1)) % nz if way == 0 else s - 1
        dst = nz - s if way == 0 else s
        first, size = p.agcut[half]
        n = p.ag.index((way, half, s))
        return remote(
            tok(src).at[pl.ds(first, size)],
            tok(dst).at[pl.ds(first, size)],
            ags.at[n],
            agr.at[n],
            right if way == 0 else left,
        )

    agc = {}

    def ag_start(s):
        for way, half, step in p.ag:
            if step == s:
                if s > 1:
                    agc[way, half, s - 1].wait_recv()
                agc[way, half, s] = go(ag_copy(way, half, s))
        if s == p.half:
            for way in (0, 1):
                if s > 1:
                    agc[way, 1 - way, s - 1].wait_recv()

    ag_start(1)

    hd = p.d // 2
    keep = pltpu.make_async_copy(wts, wall.at[0, 0], lsem.at[0])
    keep.start()
    xc = [go(remote(wts, wall.at[0, 1], xs.at[0], xr.at[0], twin))]
    if nx > 1:
        xc.append(go(remote(wts, wall.at[3, 0], xs.at[1], xr.at[1], xright)))
        xc.append(go(remote(wts, wall.at[1, 0], xs.at[2], xr.at[2], xleft)))

    keep_piece = pltpu.make_async_copy(block.at[y], spread.at[y], lsem.at[1])
    keep_piece.start()
    sc = [
        go(remote(block.at[(y + j) % ny], spread.at[y], ss.at[j - 1], sr.at[j - 1], above[j]))
        for j in range(1, ny)
    ]

    def spread_ready():
        keep_piece.wait()
        for copy in sc:
            copy.wait_recv()

    cc = {}

    def convey(t):
        for lane in (0, 1):
            for way in (0, 1):
                n = (way * 2 + lane) * p.steps + t
                c = (way * 2 + lane) * 3
                if t > 0:
                    for inlane in (0, 1):
                        if (way, inlane, t - 1) not in arrived:
                            cc[way, inlane, t - 1].wait_recv()
                            arrived.add((way, inlane, t - 1))
                    value = jnp.where(
                        ctl[c + 2] == 1, cin[(way * 2 + 1) * p.steps + t - 1], cin[way * 2 * p.steps + t - 1]
                    )
                    if t < p.chunks:
                        value = jnp.where(ctl[c] == 1, spread[ctl[c + 1], pl.ds(t * p.chunk, p.chunk)], value)
                else:
                    value = spread[ctl[c + 1], pl.ds(0, p.chunk)]
                cout[n] = value
                cc[way, lane, t] = go(
                    remote(cout.at[n], cin.at[n], cs.at[n], cr.at[n], right if way == 0 else left)
                )

    arrived = set()
    todo = list(range(p.steps))

    def convey_next(count=1):
        for _ in range(count):
            if todo:
                convey(todo.pop(0))

    fc = []

    def deliver():
        for way in (0, 1):
            for lane in (0, 1):
                cc[way, lane, p.steps - 1].wait_recv()
        for j in list(range(1, ny)) + [0]:
            c = 12 + ((y + j) % ny) * 4
            kind, ysrc, lane, skew = ctl[c], ctl[c + 1], ctl[c + 2], ctl[c + 3]
            from_cw = lane * p.steps + skew
            from_ccw = (2 + lane) * p.steps + skew

            def one(k, carry):
                rows = pl.ds(pl.multiple_of(k * p.chunk, p.chunk), p.chunk)
                value = jnp.where(kind == 1, cin[from_cw + k], cin[from_ccw + k])
                fin[j, rows] = jnp.where(kind == 0, spread[ysrc, rows], value)
                return carry

            lax.fori_loop(0, p.chunks, one, 0)
            if j == 0:
                own = pltpu.make_async_copy(fin.at[0], moved.at[y], lsem.at[2])
                own.start()
                fc.append(own)
            else:
                fc.append(go(remote(fin.at[j], moved.at[y], fs.at[j - 1], fr.at[j - 1], above[j])))

    def delivered():
        for copy in fc[:-1]:
            copy.wait_recv()
        fc[-1].wait()

    def x_second():
        if nx > 1:
            lo, hi = pl.ds(0, hd), pl.ds(hd, hd)
            xc[1].wait_recv()
            xc.append(go(remote(wall.at[3, 0, :, lo], wall.at[2, 0, :, lo], xs.at[3], xr.at[3], xright)))
            xc.append(go(remote(wall.at[3, 0], wall.at[3, 1], xs.at[4], xr.at[4], twin)))
            xc[2].wait_recv()
            xc.append(go(remote(wall.at[1, 0, :, hi], wall.at[2, 0, :, hi], xs.at[5], xr.at[5], xleft)))
            xc.append(go(remote(wall.at[1, 0], wall.at[1, 1], xs.at[6], xr.at[6], twin)))

    def x_third():
        if nx > 1:
            xc[3].wait_recv()
            xc[5].wait_recv()
            xc.append(go(remote(wall.at[2, 0], wall.at[2, 1], xs.at[7], xr.at[7], twin)))

    def x_ready():
        keep.wait()
        xc[0].wait_recv()
        if nx > 1:
            for n in (4, 6, 7):
                xc[n].wait_recv()

    tok_n = p.tok
    ta = lax.broadcasted_iota(jnp.int32, (tok_n, tok_n), 0)
    tb = lax.broadcasted_iota(jnp.int32, (tok_n, tok_n), 1)
    before = (ta < tb).astype(F32).astype(BF16)
    after = (tb < ta).astype(F32).astype(BF16)
    same = (ta == tb).astype(F32).astype(BF16)
    jrow = lax.broadcasted_iota(jnp.int32, (8, 1), 0)
    yrow = jnp.where(jrow + y >= ny, jrow + y - ny, jrow + y)
    column = jnp.where(jrow < ny, yrow * nz + z, -5).astype(F32)
    nt = (((1,), (1,)), ((), ()))

    def places(r):
        m = tok(r)[pl.ds(tok_n, META), pl.ds(0, tok_n)].astype(F32)
        named = jnp.zeros((8, tok_n), F32)
        ghi = jnp.zeros((8, tok_n), F32)
        glo = jnp.zeros((8, tok_n), F32)
        for k in range(4):
            hit = m[k : k + 1] == column
            named = named + jnp.where(hit, 1.0, 0.0)
            ghi = ghi + jnp.where(hit, m[4 + k : 5 + k], 0.0)
            glo = glo + jnp.where(hit, m[8 + k : 9 + k], 0.0)
        nb = named.astype(BF16)
        rank = jnp.dot(nb, before, preferred_element_type=F32)
        prow[r] = jnp.where(named > 0.5, rank, -4096.0)
        rank_c = lax.dot_general(after, nb, nt, preferred_element_type=F32)
        named_c = lax.dot_general(same, nb, nt, preferred_element_type=F32)
        gate_c = lax.dot_general(same, ghi.astype(BF16), nt, preferred_element_type=F32) + lax.dot_general(
            same, glo.astype(BF16), nt, preferred_element_type=F32
        )
        pcol[r, :, pl.ds(0, 8)] = jnp.where(named_c > 0.5, rank_c, -4096.0)
        pcol[r, :, pl.ds(8, 8)] = gate_c

    crow = lax.broadcasted_iota(jnp.int32, (p.rows, tok_n), 0).astype(F32)
    dc = {}
    nslot = 2 * ny

    def dispatch(h):
        for j in list(range(1, ny)) + [0]:
            total = jnp.zeros((p.rows, p.d), F32)
            for i, r in enumerate(p.groups[h]):
                pick = jnp.where(prow[r, j : j + 1, :] + float(i * p.cap) == crow, 1.0, 0.0).astype(BF16)
                total = total + jnp.dot(pick, tok(r)[pl.ds(0, tok_n)], preferred_element_type=F32)
            total = total.astype(BF16)
            if j == 0:
                recvd[pl.ds(h * ny * p.rows, p.rows)] = total
            else:
                n = h * (ny - 1) + j - 1
                sendb[n] = total
                pos = p.yorder.index((ny - j) % ny)
                dc[h, pos] = go(
                    remote(
                        sendb.at[n], recvd.at[pl.ds((h * ny + pos) * p.rows, p.rows)], ds.at[n], dr.at[n], above[j]
                    )
                )

    ec = {}

    def expert(h, first, count):
        base = (h * ny + first) * p.rows
        size = count * p.rows
        for pos in range(first, first + count):
            if pos > 0:
                dc[h, pos].wait_recv()

        def chunk(c, carry):
            xin = recvd[pl.ds(base, size)]
            wg = jnp.concatenate([wall[c, 0, 0], wall[c, 1, 0]], axis=1)
            wu = jnp.concatenate([wall[c, 0, 1], wall[c, 1, 1]], axis=1)
            wd = jnp.concatenate([wall[c, 0, 2], wall[c, 1, 2]], axis=1)
            g = jnp.dot(xin, wg, preferred_element_type=F32)
            u = jnp.dot(xin, wu, preferred_element_type=F32)
            hid = (g / (1.0 + jnp.exp(-g)) * u).astype(BF16)
            add = lax.dot_general(hid, wd, nt, preferred_element_type=F32)
            acc[pl.ds(0, size)] = acc[pl.ds(0, size)] + add
            return carry

        acc[pl.ds(0, size)] = jnp.zeros((size, p.d), F32)
        lax.fori_loop(0, nx, chunk, 0)
        res[pl.ds(base, size)] = acc[pl.ds(0, size)].astype(BF16)
        for pos in range(first, first + count):
            if pos > 0:
                o = p.yorder[pos]
                j = ny - o
                n = h * (ny - 1) + j - 1
                ec[h, j] = go(
                    remote(
                        res.at[pl.ds((h * ny + pos) * p.rows, p.rows)], rret.at[n], es.at[n], er.at[n], above[o]
                    )
                )

    ccol = lax.broadcasted_iota(jnp.int32, (tok_n, p.rows), 1).astype(F32)

    def combine(r):
        h = 0 if r in p.groups[0] else 1
        i = p.groups[h].index(r)
        total = jnp.zeros((tok_n, p.d), F32)
        for j in range(ny):
            pick = jnp.where(pcol[r, :, j : j + 1] + float(i * p.cap) == ccol, 1.0, 0.0).astype(BF16)
            rows = res[pl.ds(h * ny * p.rows, p.rows)] if j == 0 else rret[h * (ny - 1) + j - 1]
            total = total + pcol[r, :, 8 + j : 9 + j] * jnp.dot(pick, rows, preferred_element_type=F32)
        part[r] = total

    places(0)
    for s in range(2, p.half):
        ag_start(s)
        places(s - 1)
        places(nz - s + 1)
    ag_start(p.half)
    places(p.half - 1)
    places(nz - p.half + 1)
    dispatch(0)
    x_second()
    spread_ready()
    for way in (0, 1):
        agc[way, way, p.half].wait_recv()
    places(p.half)
    convey_next()
    dispatch(1)
    convey_next()
    x_third()
    x_ready()
    for h in (0, 1):
        for first in range(0, ny, 2):
            expert(h, first, min(2, ny - first))
            convey_next()
    for h in (0, 1):
        for j in range(1, ny):
            ec[h, j].wait_recv()
        for r in sorted(p.groups[h], key=lambda r: -min(r, nz - r)):
            combine(r)
            convey_next()
    convey_next(len(todo))
    deliver()

    rc = {}
    for way, half, dist in p.rs:
        n = p.rs.index((way, half, dist))
        first, size = p.rscut[half]
        off = dist if way == 0 else nz - dist
        total = part[off, pl.ds(first, size)]
        if (way, half, dist + 1) in rc:
            rc[way, half, dist + 1].wait_recv()
            total = total + rsin[p.rs.index((way, half, dist + 1)), pl.ds(0, size)].astype(F32)
        rsout[n, pl.ds(0, size)] = total.astype(BF16)
        rc[way, half, dist] = go(
            remote(
                rsout.at[n, pl.ds(0, size)],
                rsin.at[n, pl.ds(0, size)],
                rss.at[n],
                rsr.at[n],
                right if way == 0 else left,
            )
        )
    for half in (0, 1):
        first, size = p.rscut[half]
        total = part[0, pl.ds(first, size)]
        for way in (0, 1):
            rc[way, half, 1].wait_recv()
            total = total + rsin[p.rs.index((way, half, 1)), pl.ds(0, size)].astype(F32)
        out[pl.ds(first, size)] = total.astype(BF16)
    delivered()
    for copy in started:
        copy.wait_send()


def moe(p, tokx, weights, block, ctl):
    ny, nz, nx = p.ny, p.nz, p.nx
    dma = pltpu.SemaphoreType.DMA
    return pl.pallas_call(
        functools.partial(moe_kernel, p),
        out_shape=(
            jax.ShapeDtypeStruct((p.tok, p.d), BF16),
            jax.ShapeDtypeStruct((ny, p.piece, p.hs), BF16),
        ),
        in_specs=[
            pl.BlockSpec(memory_space=pltpu.VMEM),
            pl.BlockSpec(memory_space=pl.ANY),
            pl.BlockSpec(memory_space=pl.ANY),
            pl.BlockSpec(memory_space=pltpu.SMEM),
        ],
        out_specs=(pl.BlockSpec(memory_space=pltpu.VMEM), pl.BlockSpec(memory_space=pl.ANY)),
        scratch_shapes=[
            pltpu.VMEM((nz - 1, p.tok + META, p.d), BF16),
            pltpu.VMEM((2 * (ny - 1), p.rows, p.d), BF16),
            pltpu.VMEM((2 * ny * p.rows, p.d), BF16),
            pltpu.VMEM((nx, 2, 3, p.d, p.hs), BF16),
            pltpu.VMEM((2 * ny * p.rows, p.d), BF16),
            pltpu.VMEM((2 * (ny - 1), p.rows, p.d), BF16),
            pltpu.VMEM((nz, p.tok, p.d), F32),
            pltpu.VMEM((len(p.rs), p.tok // 2, p.d), BF16),
            pltpu.VMEM((len(p.rs), p.tok // 2, p.d), BF16),
            pltpu.VMEM((2 * p.rows, p.d), F32),
            pltpu.VMEM((nz, 8, p.tok), F32),
            pltpu.VMEM((nz, p.tok, 128), F32),
            pltpu.VMEM((ny, p.piece, p.hs), BF16),
            pltpu.VMEM((4 * p.steps, p.chunk, p.hs), BF16),
            pltpu.VMEM((4 * p.steps, p.chunk, p.hs), BF16),
            pltpu.VMEM((ny, p.piece, p.hs), BF16),
            dma((3,)),
            dma((len(p.ag),)),
            dma((len(p.ag),)),
            dma((8,)),
            dma((8,)),
            dma((2 * (ny - 1),)),
            dma((2 * (ny - 1),)),
            dma((2 * (ny - 1),)),
            dma((2 * (ny - 1),)),
            dma((len(p.rs),)),
            dma((len(p.rs),)),
            dma((ny - 1,)),
            dma((ny - 1,)),
            dma((4 * p.steps,)),
            dma((4 * p.steps,)),
            dma((ny - 1,)),
            dma((ny - 1,)),
        ],
        compiler_params=pltpu.CompilerParams(
            collective_id=0, has_side_effects=True, vmem_limit_bytes=60 * 1024 * 1024
        ),
        name="moe",
    )(tokx, weights, block, ctl)


def routes(p, source_slot):
    nz = p.nz
    ex = lax.axis_index("expert")
    z = ex % nz
    slot = jnp.arange(p.ny * nz, dtype=jnp.int32)
    zs, ys, zd = source_slot % nz, source_slot // nz, slot % nz
    ahead = (zd - zs + nz) % nz
    far = (ahead, (nz - ahead) % nz)
    goes = ((ahead >= 1) & (ahead <= p.half), ahead > p.half)
    earlier = slot[None, :] < slot[:, None]

    def lanes(way, at):
        passed = (at - zs + 2 * nz) % nz if way == 0 else (zs - at + 2 * nz) % nz
        on = goes[way] & (passed < far[way])
        return on, jnp.sum((earlier & on[None, :]).astype(jnp.int32), axis=1)

    numbers = []
    into = []
    for way in (0, 1):
        on_out, lane_out = lanes(way, z)
        _, lane_in = lanes(way, z - 1 if way == 0 else z + 1)
        into.append(lane_in)
        for lane in (0, 1):
            this = on_out & (lane_out == lane)
            for what in ((zs == z).astype(jnp.int32), ys, lane_in):
                numbers.append(jnp.sum(jnp.where(this, what, 0)))
    kind = jnp.where(goes[0], 1, jnp.where(goes[1], 2, 0))
    lane = jnp.where(goes[0], into[0], jnp.where(goes[1], into[1], 0))
    skew = jnp.where(goes[0], far[0] - 1, jnp.where(goes[1], far[1] - 1, 0))
    table = jnp.stack([kind, ys, lane, skew], axis=1).reshape(p.ny, nz, 4)
    mine = jnp.sum(jnp.where((jnp.arange(nz) == z)[None, :, None], table, 0), axis=1)
    return jnp.concatenate([jnp.stack(numbers), mine.reshape(-1)]).astype(jnp.int32)


def per_device(n_y, tokens, route_ids, gate_weight, old_owner, new_owner, weights, first_moment, second_moment):
    n = lax.axis_size("expert")
    tok, d = tokens.shape
    p = Plan(lax.axis_size("dp"), n_y, n // n_y, tok, 3 * tok * route_ids.shape[1] // (2 * n), d, weights.shape[3])
    labels = jnp.arange(n, dtype=jnp.int32)
    source_slot = jnp.sum(jnp.where(new_owner[None, :] == labels[:, None], old_owner[None, :], 0), axis=1)
    slots = jnp.sum(jnp.where(route_ids[:, :, None] == labels, old_owner, 0), axis=2)
    high = lax.reduce_precision(gate_weight, 8, 7)
    meta = jnp.concatenate([slots.astype(F32), high, gate_weight - high, jnp.full((tok, META - 12), -1.0, F32)], axis=1)
    meta = jnp.pad(meta.T.astype(BF16), ((0, 0), (0, d - tok)))
    tokx = jnp.concatenate([tokens, meta], axis=0)
    block = jnp.concatenate([weights[0], first_moment[0].astype(BF16), second_moment[0].astype(BF16)], axis=0)
    layer_output, moved = moe(
        p, tokx, weights[0], block.reshape(p.ny, p.piece, p.hs), routes(p, source_slot)
    )
    moved = moved.reshape((1, *block.shape))
    me = lax.axis_index("expert")
    stays = jnp.sum(jnp.where(labels == me, source_slot, 0)) == me
    return (
        layer_output,
        jnp.where(stays, weights, moved[:, 0:3]),
        jnp.where(stays, first_moment, moved[:, 3:6].astype(F32)),
        jnp.where(stays, second_moment, moved[:, 6:9].astype(F32)),
    )


def solution(mesh):
    experts = mesh.shape["expert"]
    n_y = 4 if experts == 32 else 2
    placed = (
        P(("dp", "expert"), None),
        P(("dp", "expert"), None),
        P(("dp", "expert"), None),
        P(),
        P(),
        P("expert", None, None, "dp"),
        P("expert", None, None, "dp"),
        P("expert", None, None, "dp"),
    )
    return jax.shard_map(
        functools.partial(per_device, n_y),
        mesh=mesh,
        in_specs=placed,
        out_specs=(
            P(("dp", "expert"), None),
            P("expert", None, None, "dp"),
            P("expert", None, None, "dp"),
            P("expert", None, None, "dp"),
        ),
        check_vma=False,
    )
```

```python
import functools

import jax
import jax.numpy as jnp
from jax import lax
from jax.experimental import pallas as pl
from jax.experimental.pallas import tpu as pltpu
from jax.sharding import PartitionSpec as P

MESH = pl.DeviceIdType.MESH
F32 = jnp.float32
BF16 = jnp.bfloat16
META = 16


class Plan:
    def __init__(self, n_dp, n_y, n_z, tok, cap, d, hs):
        self.nx, self.ny, self.nz = n_dp // 2, n_y, n_z
        self.tok, self.cap, self.d, self.hs = tok, cap, d, hs
        self.half = n_z // 2
        order = [0]
        for s in range(1, self.half):
            order += [s, n_z - s]
        order += [self.half]
        self.groups = (order[: self.half], order[self.half :])
        self.rows = self.half * cap
        self.yorder = [0, 1, 3, 2] if n_y == 4 else list(range(n_y))
        self.chunks = 8
        self.steps = self.chunks + self.half - 1
        self.piece = 9 * d // n_y
        self.chunk = self.piece // self.chunks
        cut = tok // 2
        self.agcut = ((0, cut), (cut, tok + META - cut))
        self.rscut = ((0, cut), (cut, tok - cut))
        self.ag = [
            (way, part, s)
            for s in range(1, self.half + 1)
            for way in (0, 1)
            for part in (0, 1)
            if s < self.half or way == part
        ]
        self.rs = [
            (way, part, dist)
            for dist in range(self.half, 0, -1)
            for way in (0, 1)
            for part in (0, 1)
            if dist < self.half or way == part
        ]


class Link:
    def __init__(self, src, dst, send, recv, to):
        self.copy = pltpu.make_async_remote_copy(
            src_ref=src, dst_ref=dst, send_sem=send, recv_sem=recv, device_id=to, device_id_type=MESH
        )
        self.copy.start()
        self.here = False

    def arrive(self):
        if not self.here:
            self.copy.wait_recv()
            self.here = True


def moe_kernel(
    p,
    tokens,
    route,
    gate,
    old,
    new,
    wts,
    first_m,
    second_m,
    out,
    moved,
    tokb,
    sendb,
    recvd,
    wall,
    res,
    rret,
    part,
    rsin,
    rsout,
    acc,
    prow,
    pcol,
    stage,
    block,
    spread,
    cin,
    cout,
    fin,
    lsem,
    ags,
    agr,
    xs,
    xr,
    ds,
    dr,
    es,
    er,
    rss,
    rsr,
    ss,
    sr,
    cs,
    cr,
    fs,
    fr,
):
    ny, nz, nx = p.ny, p.nz, p.nx
    tok_n = p.tok
    dp = lax.axis_index("dp")
    ex = lax.axis_index("expert")
    x, core = dp // 2, dp % 2
    y, z = ex // nz, ex % nz
    right = (dp, y * nz + (z + 1) % nz)
    left = (dp, y * nz + (z + nz - 1) % nz)
    along = (right, left)
    above = [None] + [(dp, ((y + j) % ny) * nz + z) for j in range(1, ny)]
    twin = (x * 2 + 1 - core, ex)
    xright = (((x + 1) % nx) * 2 + core, ex)
    xleft = (((x + nx - 1) % nx) * 2 + core, ex)
    started = []

    def go(*what):
        link = Link(*what)
        started.append(link)
        return link

    def local(n, src, dst):
        copy = pltpu.make_async_copy(src, dst, lsem.at[n])
        copy.start()
        return copy

    own_tokens = local(0, tokens, tokb.at[0, pl.ds(0, tok_n)])
    own_weights = local(1, wts, wall.at[0, 0])
    wrows = 3 * p.d
    block_weights = local(2, wts, block.at[pl.ds(0, wrows)])
    stage_first = local(3, first_m, stage.at[0])
    stage_second = local(4, second_m, stage.at[1])

    barrier = pltpu.get_barrier_semaphore()
    peers = [right, left, twin] + above[1:] + ([xright, xleft] if nx > 1 else [])
    for peer in peers:
        pl.semaphore_signal(barrier, inc=1, device_id=peer, device_id_type=MESH)
    pl.semaphore_wait(barrier, len(peers))

    agc = {}

    def ag_send(way, half, s):
        src = (nz - (s - 1)) % nz if way == 0 else s - 1
        dst = nz - s if way == 0 else s
        rows = pl.ds(*p.agcut[half])
        n = p.ag.index((way, half, s))
        source = tokens.at[rows] if (s, half) == (1, 0) else tokb.at[src, rows]
        agc[way, half, s] = go(source, tokb.at[dst, rows], ags.at[n], agr.at[n], along[way])

    def ag_step(s):
        for way, half, step in p.ag:
            if step == s:
                agc[way, half, s - 1].arrive()
                ag_send(way, half, s)
        for way, half, step in p.ag:
            if step == s - 1:
                agc[way, half, step].arrive()

    for way in (0, 1):
        ag_send(way, 0, 1)

    xc = [go(wts, wall.at[0, 1], xs.at[0], xr.at[0], twin)]
    if nx > 1:
        xc.append(go(wts, wall.at[3, 0], xs.at[1], xr.at[1], xright))
        xc.append(go(wts, wall.at[1, 0], xs.at[2], xr.at[2], xleft))

    def x_second():
        if nx > 1:
            lo, hi = pl.ds(0, wrows // 2), pl.ds(wrows // 2, wrows // 2)
            xc[1].arrive()
            xc.append(go(wall.at[3, 0, lo], wall.at[2, 0, lo], xs.at[3], xr.at[3], xright))
            xc.append(go(wall.at[3, 0], wall.at[3, 1], xs.at[4], xr.at[4], twin))
            xc[2].arrive()
            xc.append(go(wall.at[1, 0, hi], wall.at[2, 0, hi], xs.at[5], xr.at[5], xleft))
            xc.append(go(wall.at[1, 0], wall.at[1, 1], xs.at[6], xr.at[6], twin))

    def x_third():
        if nx > 1:
            xc[3].arrive()
            xc[5].arrive()
            xc.append(go(wall.at[2, 0], wall.at[2, 1], xs.at[7], xr.at[7], twin))

    def x_ready():
        own_weights.wait()
        for link in xc:
            link.arrive()

    slots = jnp.zeros((4, tok_n), jnp.int32)
    for e in range(ny * nz):
        slots = jnp.where(route[...] == e, old[e], slots)
    g = gate[...]
    high = g.astype(BF16).astype(F32)
    meta = jnp.concatenate([slots.astype(F32), high, g - high, jnp.full((4, tok_n), -1.0, F32)], axis=0)
    wide = -(-tok_n // 128) * 128
    if wide > tok_n:
        meta = jnp.concatenate([meta, jnp.zeros((META, wide - tok_n), F32)], axis=1)
    tokb[0, pl.ds(tok_n, META), pl.ds(0, wide)] = meta.astype(BF16)
    if wide < p.d:
        tokb[0, pl.ds(tok_n, META), pl.ds(wide, p.d - wide)] = jnp.zeros((META, p.d - wide), BF16)
    own_tokens.wait()
    for way in (0, 1):
        ag_send(way, 1, 1)

    block_weights.wait()
    stage_first.wait()
    stage_second.wait()
    step_rows = 256

    def narrow(i, carry):
        for a in (0, 1):
            rows = pl.ds(pl.multiple_of(i * step_rows, step_rows), step_rows)
            to = pl.ds(pl.multiple_of((1 + a) * wrows + i * step_rows, step_rows), step_rows)
            block[to] = stage[a, rows].astype(BF16)
        return carry

    lax.fori_loop(0, wrows // step_rows, narrow, 0)

    def piece(i):
        return block.at[pl.ds(pl.multiple_of(i * p.piece, p.piece), p.piece)]

    keep_piece = local(5, piece(y), spread.at[y])
    sc = [go(piece((y + j) % ny), spread.at[y], ss.at[j - 1], sr.at[j - 1], above[j]) for j in range(1, ny)]

    def spread_ready():
        keep_piece.wait()
        for link in sc:
            link.arrive()

    def scan(e, carry):
        seen, named = carry
        zs, zd = old[e] % nz, new[e] % nz
        ahead = (zd - zs + nz) % nz
        seen = list(seen)
        for way in (0, 1):
            goes = (ahead >= 1) & (ahead <= p.half) if way == 0 else ahead > p.half
            far = ahead if way == 0 else nz - ahead
            for into in (0, 1):
                at = z + nz - into if way == 0 else z + into
                passed = (at - zs + nz) % nz if way == 0 else (zs - at + 2 * nz) % nz
                on = goes & (passed < far)
                n = (way * 2 + into) * 2
                seen[n] = jnp.where(on & (seen[n] < 0), e, seen[n])
                seen[n + 1] = jnp.where(on, e, seen[n + 1])
        named = tuple(jnp.where(new[e] == yy * nz + z, e, named[yy]) for yy in range(ny))
        return tuple(seen), named

    none = jnp.int32(-1)
    seen, named = lax.fori_loop(0, ny * nz, scan, ((none,) * 8, (none,) * ny))
    lanes = {}
    for way in (0, 1):
        for lane in (0, 1):
            e = jnp.maximum(seen[way * 4 + lane], 0)
            lanes[way, lane] = (old[e] % nz == z, old[e] // nz, e != seen[way * 4 + 2])
    finals = []
    for yy in range(ny):
        e = jnp.maximum(named[yy], 0)
        ahead = (new[e] % nz - old[e] % nz + nz) % nz
        by_cw = ahead <= p.half
        lane = jnp.where(e != jnp.where(by_cw, seen[2], seen[6]), 1, 0)
        skew = jnp.maximum(jnp.where(by_cw, ahead, nz - ahead) - 1, 0)
        finals.append((ahead == 0, by_cw, old[e] // nz, lane * p.steps + skew))

    cc = {}
    todo = list(range(p.steps))

    def convey(t):
        for lane in (0, 1):
            for way in (0, 1):
                n = (way * 2 + lane) * p.steps + t
                mine, ysrc, second = lanes[way, lane]
                if t > 0:
                    for inlane in (0, 1):
                        cc[way, inlane, t - 1].arrive()
                    value = jnp.where(second, cin[(way * 2 + 1) * p.steps + t - 1], cin[way * 2 * p.steps + t - 1])
                    if t < p.chunks:
                        value = jnp.where(mine, spread[ysrc, pl.ds(t * p.chunk, p.chunk)], value)
                else:
                    value = spread[ysrc, pl.ds(0, p.chunk)]
                cout[n] = value
                cc[way, lane, t] = go(cout.at[n], cin.at[n], cs.at[n], cr.at[n], along[way])

    def convey_next(count=1):
        for _ in range(count):
            if todo:
                convey(todo.pop(0))

    def choose(ny_first):
        for way in (0, 1):
            for lane in (0, 1):
                cc[way, lane, p.steps - 1].arrive()
        for j in ny_first:
            stay, by_cw, ysrc, at = finals[0]
            for yy in range(1, ny):
                here = (y + j) % ny == yy
                other = finals[yy]
                stay = (here & other[0]) | (~here & stay)
                by_cw = (here & other[1]) | (~here & by_cw)
                ysrc = jnp.where(here, other[2], ysrc)
                at = jnp.where(here, other[3], at)

            def one(k, carry):
                rows = pl.ds(pl.multiple_of(k * p.chunk, p.chunk), p.chunk)
                value = jnp.where(by_cw, cin[at + k], cin[2 * p.steps + at + k])
                fin[j, rows] = jnp.where(stay, spread[ysrc, rows], value)
                return carry

            lax.fori_loop(0, p.chunks, one, 0)

    fc = []

    def deliver():
        for j in range(1, ny):
            fc.append(go(fin.at[j], moved.at[y], fs.at[j - 1], fr.at[j - 1], above[j]))
        fc.append(local(6, fin.at[0], moved.at[y]))

    ta = lax.broadcasted_iota(jnp.int32, (tok_n, tok_n), 0)
    tb = lax.broadcasted_iota(jnp.int32, (tok_n, tok_n), 1)
    before = (ta < tb).astype(F32).astype(BF16)
    after = (tb < ta).astype(F32).astype(BF16)
    same = (ta == tb).astype(F32).astype(BF16)
    jrow = lax.broadcasted_iota(jnp.int32, (8, 1), 0)
    yrow = jnp.where(jrow + y >= ny, jrow + y - ny, jrow + y)
    column = jnp.where(jrow < ny, yrow * nz + z, -5).astype(F32)
    nt = (((1,), (1,)), ((), ()))

    def places(r):
        m = tokb[r, pl.ds(tok_n, META), pl.ds(0, tok_n)].astype(F32)
        named = jnp.zeros((8, tok_n), F32)
        ghi = jnp.zeros((8, tok_n), F32)
        glo = jnp.zeros((8, tok_n), F32)
        for k in range(4):
            hit = m[k : k + 1] == column
            named = named + jnp.where(hit, 1.0, 0.0)
            ghi = ghi + jnp.where(hit, m[4 + k : 5 + k], 0.0)
            glo = glo + jnp.where(hit, m[8 + k : 9 + k], 0.0)
        nb = named.astype(BF16)
        rank = jnp.dot(nb, before, preferred_element_type=F32)
        prow[r] = jnp.where(named > 0.5, rank, -4096.0)
        rank_c = lax.dot_general(after, nb, nt, preferred_element_type=F32)
        named_c = lax.dot_general(same, nb, nt, preferred_element_type=F32)
        gate_c = lax.dot_general(same, ghi.astype(BF16), nt, preferred_element_type=F32) + lax.dot_general(
            same, glo.astype(BF16), nt, preferred_element_type=F32
        )
        pcol[r, :, pl.ds(0, 8)] = jnp.where(named_c > 0.5, rank_c, -4096.0)
        pcol[r, :, pl.ds(8, 8)] = gate_c

    crow = lax.broadcasted_iota(jnp.int32, (p.rows, tok_n), 0).astype(F32)
    dc = {}

    def dispatch(h):
        for j in list(range(1, ny)) + [0]:
            total = jnp.zeros((p.rows, p.d), F32)
            for i, r in enumerate(p.groups[h]):
                pick = jnp.where(prow[r, j : j + 1, :] + float(i * p.cap) == crow, 1.0, 0.0).astype(BF16)
                total = total + jnp.dot(pick, tokb[r, pl.ds(0, tok_n)], preferred_element_type=F32)
            total = total.astype(BF16)
            if j == 0:
                recvd[pl.ds(h * ny * p.rows, p.rows)] = total
            else:
                n = h * (ny - 1) + j - 1
                sendb[n] = total
                pos = p.yorder.index((ny - j) % ny)
                at = pl.ds((h * ny + pos) * p.rows, p.rows)
                dc[h, pos] = go(sendb.at[n], recvd.at[at], ds.at[n], dr.at[n], above[j])

    ec = {}

    def expert(h, first, count):
        base = (h * ny + first) * p.rows
        size = count * p.rows
        for pos in range(first, first + count):
            if pos > 0:
                dc[h, pos].arrive()

        def matrix(c, i):
            rows = pl.ds(i * p.d, p.d)
            return jnp.concatenate([wall[c, 0, rows], wall[c, 1, rows]], axis=1)

        def chunk(c, carry):
            xin = recvd[pl.ds(base, size)]
            g = jnp.dot(xin, matrix(c, 0), preferred_element_type=F32)
            u = jnp.dot(xin, matrix(c, 1), preferred_element_type=F32)
            hid = (g / (1.0 + jnp.exp(-g)) * u).astype(BF16)
            add = lax.dot_general(hid, matrix(c, 2), nt, preferred_element_type=F32)
            acc[pl.ds(0, size)] = acc[pl.ds(0, size)] + add
            return carry

        acc[pl.ds(0, size)] = jnp.zeros((size, p.d), F32)
        lax.fori_loop(0, nx, chunk, 0)
        res[pl.ds(base, size)] = acc[pl.ds(0, size)].astype(BF16)
        for pos in range(first, first + count):
            if pos > 0:
                o = p.yorder[pos]
                j = ny - o
                n = h * (ny - 1) + j - 1
                at = pl.ds((h * ny + pos) * p.rows, p.rows)
                ec[h, j] = go(res.at[at], rret.at[n], es.at[n], er.at[n], above[o])

    ccol = lax.broadcasted_iota(jnp.int32, (tok_n, p.rows), 1).astype(F32)

    def combine(r):
        h = 0 if r in p.groups[0] else 1
        i = p.groups[h].index(r)
        total = jnp.zeros((tok_n, p.d), F32)
        for j in range(ny):
            pick = jnp.where(pcol[r, :, j : j + 1] + float(i * p.cap) == ccol, 1.0, 0.0).astype(BF16)
            rows = res[pl.ds(h * ny * p.rows, p.rows)] if j == 0 else rret[h * (ny - 1) + j - 1]
            total = total + pcol[r, :, 8 + j : 9 + j] * jnp.dot(pick, rows, preferred_element_type=F32)
        part[r] = total

    rc = {}

    def reduce_step(dist):
        for way, half, d in p.rs:
            if d == dist:
                n = p.rs.index((way, half, dist))
                first, size = p.rscut[half]
                total = part[dist if way == 0 else nz - dist, pl.ds(first, size)]
                if (way, half, dist + 1) in rc:
                    rc[way, half, dist + 1].arrive()
                    total = total + rsin[p.rs.index((way, half, dist + 1)), pl.ds(0, size)].astype(F32)
                rsout[n, pl.ds(0, size)] = total.astype(BF16)
                rows = pl.ds(0, size)
                rc[way, half, dist] = go(rsout.at[n, rows], rsin.at[n, rows], rss.at[n], rsr.at[n], along[way])

    places(0)
    for s in range(2, p.half + 1):
        ag_step(s)
        places(s - 1)
        places(nz - s + 1)
    dispatch(0)
    x_second()
    spread_ready()
    for way in (0, 1):
        agc[way, way, p.half].arrive()
    places(p.half)
    convey_next()
    dispatch(1)
    convey_next()
    x_third()
    x_ready()
    for h in (0, 1):
        for first in range(0, ny, 2):
            expert(h, first, min(2, ny - first))
            convey_next()
    for j in range(1, ny):
        ec[0, j].arrive()
    for r in p.groups[0]:
        combine(r)
        convey_next()
    convey_next(len(todo))
    choose(range(ny))
    for j in range(1, ny):
        ec[1, j].arrive()
    deliver()
    for dist in range(p.half, 0, -1):
        for r in sorted({dist, nz - dist}):
            if r in p.groups[1]:
                combine(r)
        reduce_step(dist)
    for half in (0, 1):
        first, size = p.rscut[half]
        total = part[0, pl.ds(first, size)]
        for way in (0, 1):
            rc[way, half, 1].arrive()
            total = total + rsin[p.rs.index((way, half, 1)), pl.ds(0, size)].astype(F32)
        out[pl.ds(first, size)] = total.astype(BF16)
    for link in started:
        link.arrive()
    fc[-1].wait()
    for link in started:
        link.copy.wait_send()


def moe(p, *operands):
    ny, nz, nx = p.ny, p.nz, p.nx
    dma = pltpu.SemaphoreType.DMA
    vmem = pl.BlockSpec(memory_space=pltpu.VMEM)
    smem = pl.BlockSpec(memory_space=pltpu.SMEM)
    anywhere = pl.BlockSpec(memory_space=pl.ANY)
    wrows = 3 * p.d
    return pl.pallas_call(
        functools.partial(moe_kernel, p),
        out_shape=(
            jax.ShapeDtypeStruct((p.tok, p.d), BF16),
            jax.ShapeDtypeStruct((ny, p.piece, p.hs), BF16),
        ),
        in_specs=[anywhere, vmem, vmem, smem, smem, anywhere, anywhere, anywhere],
        out_specs=(vmem, anywhere),
        scratch_shapes=[
            pltpu.VMEM((nz, p.tok + META, p.d), BF16),
            pltpu.VMEM((2 * (ny - 1), p.rows, p.d), BF16),
            pltpu.VMEM((2 * ny * p.rows, p.d), BF16),
            pltpu.VMEM((nx, 2, wrows, p.hs), BF16),
            pltpu.VMEM((2 * ny * p.rows, p.d), BF16),
            pltpu.VMEM((2 * (ny - 1), p.rows, p.d), BF16),
            pltpu.VMEM((nz, p.tok, p.d), F32),
            pltpu.VMEM((len(p.rs), p.tok // 2, p.d), BF16),
            pltpu.VMEM((len(p.rs), p.tok // 2, p.d), BF16),
            pltpu.VMEM((2 * p.rows, p.d), F32),
            pltpu.VMEM((nz, 8, p.tok), F32),
            pltpu.VMEM((nz, p.tok, 128), F32),
            pltpu.VMEM((2, wrows, p.hs), F32),
            pltpu.VMEM((3 * wrows, p.hs), BF16),
            pltpu.VMEM((ny, p.piece, p.hs), BF16),
            pltpu.VMEM((4 * p.steps, p.chunk, p.hs), BF16),
            pltpu.VMEM((4 * p.steps, p.chunk, p.hs), BF16),
            pltpu.VMEM((ny, p.piece, p.hs), BF16),
            dma((7,)),
            dma((len(p.ag),)),
            dma((len(p.ag),)),
            dma((8,)),
            dma((8,)),
            dma((2 * (ny - 1),)),
            dma((2 * (ny - 1),)),
            dma((2 * (ny - 1),)),
            dma((2 * (ny - 1),)),
            dma((len(p.rs),)),
            dma((len(p.rs),)),
            dma((ny - 1,)),
            dma((ny - 1,)),
            dma((4 * p.steps,)),
            dma((4 * p.steps,)),
            dma((ny - 1,)),
            dma((ny - 1,)),
        ],
        compiler_params=pltpu.CompilerParams(
            collective_id=0, has_side_effects=True, vmem_limit_bytes=60 * 1024 * 1024
        ),
        name="moe",
    )(*operands)


def per_device(n_y, tokens, route_ids, gate_weight, old_owner, new_owner, weights, first_moment, second_moment):
    n = lax.axis_size("expert")
    tok, d = tokens.shape
    hs = weights.shape[3]
    p = Plan(lax.axis_size("dp"), n_y, n // n_y, tok, 3 * tok * route_ids.shape[1] // (2 * n), d, hs)
    layer_output, moved = moe(
        p,
        tokens,
        route_ids.T,
        gate_weight.T,
        old_owner,
        new_owner,
        weights.reshape(-1, hs),
        first_moment.reshape(-1, hs),
        second_moment.reshape(-1, hs),
    )
    moved = moved.reshape((3, *weights.shape))
    me = lax.axis_index("expert")
    stays = jnp.any((old_owner == me) & (new_owner == me))
    return (
        layer_output,
        jnp.where(stays, weights, moved[0]),
        jnp.where(stays, first_moment, moved[1].astype(F32)),
        jnp.where(stays, second_moment, moved[2].astype(F32)),
    )


def solution(mesh):
    experts = mesh.shape["expert"]
    n_y = 4 if experts == 32 else 2
    placed = (
        P(("dp", "expert"), None),
        P(("dp", "expert"), None),
        P(("dp", "expert"), None),
        P(),
        P(),
        P("expert", None, None, "dp"),
        P("expert", None, None, "dp"),
        P("expert", None, None, "dp"),
    )
    return jax.shard_map(
        functools.partial(per_device, n_y),
        mesh=mesh,
        in_specs=placed,
        out_specs=(
            P(("dp", "expert"), None),
            P("expert", None, None, "dp"),
            P("expert", None, None, "dp"),
            P("expert", None, None, "dp"),
        ),
        check_vma=False,
    )
```

```python
import functools

import jax
import jax.numpy as jnp
from jax import lax
from jax.experimental import pallas as pl
from jax.experimental.pallas import tpu as pltpu
from jax.sharding import PartitionSpec as P

MESH = pl.DeviceIdType.MESH
F32 = jnp.float32
BF16 = jnp.bfloat16
META = 16
FAR_FIRST = False
EARLY = False


class Plan:
    def __init__(self, n_dp, n_y, n_z, tok, cap, d, hs):
        self.nx, self.ny, self.nz = n_dp // 2, n_y, n_z
        self.tok, self.cap, self.d, self.hs = tok, cap, d, hs
        self.half = n_z // 2
        order = [0]
        for s in range(1, self.half):
            order += [s, n_z - s]
        order += [self.half]
        self.groups = (order[: self.half], order[self.half :])
        self.rows = self.half * cap
        self.yorder = [0, 1, 3, 2] if n_y == 4 else list(range(n_y))
        self.chunks = 8
        self.steps = self.chunks + self.half - 1
        self.piece = 9 * d // n_y
        self.chunk = self.piece // self.chunks
        cut = tok // 2
        self.agcut = ((0, cut), (cut, tok - cut))
        self.rscut = ((0, cut), (cut, tok - cut))
        self.ag = [
            (way, part, s)
            for s in range(1, self.half + 1)
            for part in (0, 1, 2)
            for way in (0, 1)
            if s < self.half or way == part % 2
        ]
        self.rs = [
            (way, part, dist)
            for dist in range(self.half, 0, -1)
            for part in (0, 1)
            for way in (0, 1)
            if dist < self.half or way == part
        ]


class Link:
    def __init__(self, src, dst, send, recv, to):
        self.copy = pltpu.make_async_remote_copy(
            src_ref=src, dst_ref=dst, send_sem=send, recv_sem=recv, device_id=to, device_id_type=MESH
        )
        self.copy.start()
        self.here = False

    def arrive(self):
        if not self.here:
            self.copy.wait_recv()
            self.here = True


def moe_kernel(
    p,
    tokens,
    route,
    gate,
    old,
    new,
    wts,
    first_m,
    second_m,
    out,
    moved,
    tokb,
    metab,
    sendb,
    recvd,
    wall,
    res,
    rret,
    part,
    rsin,
    rsout,
    acc,
    prow,
    pcol,
    stage,
    block,
    spread,
    cin,
    cout,
    fin,
    lsem,
    ags,
    agr,
    xs,
    xr,
    ds,
    dr,
    es,
    er,
    rss,
    rsr,
    ss,
    sr,
    cs,
    cr,
    fs,
    fr,
):
    ny, nz, nx = p.ny, p.nz, p.nx
    tok_n = p.tok
    dp = lax.axis_index("dp")
    ex = lax.axis_index("expert")
    x, core = dp // 2, dp % 2
    y, z = ex // nz, ex % nz
    right = (dp, y * nz + (z + 1) % nz)
    left = (dp, y * nz + (z + nz - 1) % nz)
    along = (right, left)
    above = [None] + [(dp, ((y + j) % ny) * nz + z) for j in range(1, ny)]
    twin = (x * 2 + 1 - core, ex)
    xright = (((x + 1) % nx) * 2 + core, ex)
    xleft = (((x + nx - 1) % nx) * 2 + core, ex)
    started = []

    def go(*what):
        link = Link(*what)
        started.append(link)
        return link

    def local(n, src, dst):
        copy = pltpu.make_async_copy(src, dst, lsem.at[n])
        copy.start()
        return copy

    own_tokens = local(0, tokens, tokb.at[0])
    own_weights = local(1, wts, wall.at[0, 0])
    wrows = 3 * p.d
    block_weights = local(2, wts, block.at[pl.ds(0, wrows)])
    stage_first = local(3, first_m, stage.at[0])
    stage_second = local(4, second_m, stage.at[1])

    barrier = pltpu.get_barrier_semaphore()
    peers = [right, left, twin] + above[1:] + ([xright, xleft] if nx > 1 else [])
    for peer in peers:
        pl.semaphore_signal(barrier, inc=1, device_id=peer, device_id_type=MESH)
    pl.semaphore_wait(barrier, len(peers))

    agc = {}

    def ag_send(way, half, s):
        src = (nz - (s - 1)) % nz if way == 0 else s - 1
        dst = nz - s if way == 0 else s
        n = p.ag.index((way, half, s))
        if half == 2:
            agc[way, half, s] = go(metab.at[src], metab.at[dst], ags.at[n], agr.at[n], along[way])
        else:
            rows = pl.ds(*p.agcut[half])
            source = tokens.at[rows] if s == 1 else tokb.at[src, rows]
            agc[way, half, s] = go(source, tokb.at[dst, rows], ags.at[n], agr.at[n], along[way])

    def ag_step(s):
        for way, half, step in p.ag:
            if step == s:
                agc[way, half, s - 1].arrive()
                ag_send(way, half, s)
        for way, half, step in p.ag:
            if step == s - 1:
                agc[way, half, step].arrive()

    for half in (0, 1):
        for way in (0, 1):
            ag_send(way, half, 1)

    xc = [go(wts, wall.at[0, 1], xs.at[0], xr.at[0], twin)]
    if nx > 1:
        xc.append(go(wts, wall.at[3, 0], xs.at[1], xr.at[1], xright))
        xc.append(go(wts, wall.at[1, 0], xs.at[2], xr.at[2], xleft))

    def x_second():
        if nx > 1:
            lo, hi = pl.ds(0, wrows // 2), pl.ds(wrows // 2, wrows // 2)
            xc[1].arrive()
            xc.append(go(wall.at[3, 0, lo], wall.at[2, 0, lo], xs.at[3], xr.at[3], xright))
            xc.append(go(wall.at[3, 0], wall.at[3, 1], xs.at[4], xr.at[4], twin))
            xc[2].arrive()
            xc.append(go(wall.at[1, 0, hi], wall.at[2, 0, hi], xs.at[5], xr.at[5], xleft))
            xc.append(go(wall.at[1, 0], wall.at[1, 1], xs.at[6], xr.at[6], twin))

    def x_third():
        if nx > 1:
            xc[3].arrive()
            xc[5].arrive()
            xc.append(go(wall.at[2, 0], wall.at[2, 1], xs.at[7], xr.at[7], twin))

    def x_ready():
        own_weights.wait()
        for link in xc:
            link.arrive()

    slots = jnp.zeros((4, tok_n), jnp.int32)
    for e in range(ny * nz):
        slots = jnp.where(route[...] == e, old[e], slots)
    g = gate[...]
    high = g.astype(BF16).astype(F32)
    meta = jnp.concatenate([slots.astype(F32), high, g - high, jnp.full((4, tok_n), -1.0, F32)], axis=0)
    wide = -(-tok_n // 128) * 128
    if wide > tok_n:
        meta = jnp.concatenate([meta, jnp.zeros((META, wide - tok_n), F32)], axis=1)
    metab[0] = meta.astype(BF16)
    for way in (0, 1):
        ag_send(way, 2, 1)

    block_weights.wait()
    stage_first.wait()
    stage_second.wait()
    step_rows = 256

    def narrow(i, carry):
        for a in (0, 1):
            rows = pl.ds(pl.multiple_of(i * step_rows, step_rows), step_rows)
            to = pl.ds(pl.multiple_of((1 + a) * wrows + i * step_rows, step_rows), step_rows)
            block[to] = stage[a, rows].astype(BF16)
        return carry

    lax.fori_loop(0, wrows // step_rows, narrow, 0)

    def piece(i):
        return block.at[pl.ds(pl.multiple_of(i * p.piece, p.piece), p.piece)]

    keep_piece = local(5, piece(y), spread.at[y])
    sc = [go(piece((y + j) % ny), spread.at[y], ss.at[j - 1], sr.at[j - 1], above[j]) for j in range(1, ny)]

    def spread_ready():
        keep_piece.wait()
        for link in sc:
            link.arrive()

    def scan(e, carry):
        seen, named = carry
        zs, zd = old[e] % nz, new[e] % nz
        ahead = (zd - zs + nz) % nz
        seen = list(seen)
        for way in (0, 1):
            goes = (ahead >= 1) & (ahead <= p.half) if way == 0 else ahead > p.half
            far = ahead if way == 0 else nz - ahead
            for into in (0, 1):
                at = z + nz - into if way == 0 else z + into
                passed = (at - zs + nz) % nz if way == 0 else (zs - at + 2 * nz) % nz
                on = goes & (passed < far)
                n = (way * 2 + into) * 2
                seen[n] = jnp.where(on & (seen[n] < 0), e, seen[n])
                seen[n + 1] = jnp.where(on, e, seen[n + 1])
        named = tuple(jnp.where(new[e] == yy * nz + z, e, named[yy]) for yy in range(ny))
        return tuple(seen), named

    none = jnp.int32(-1)
    seen, named = lax.fori_loop(0, ny * nz, scan, ((none,) * 8, (none,) * ny))
    lanes = {}
    for way in (0, 1):
        for lane in (0, 1):
            e = jnp.maximum(seen[way * 4 + lane], 0)
            lanes[way, lane] = (old[e] % nz == z, old[e] // nz, e != seen[way * 4 + 2])
    finals = []
    for yy in range(ny):
        e = jnp.maximum(named[yy], 0)
        ahead = (new[e] % nz - old[e] % nz + nz) % nz
        by_cw = ahead <= p.half
        lane = jnp.where(e != jnp.where(by_cw, seen[2], seen[6]), 1, 0)
        skew = jnp.maximum(jnp.where(by_cw, ahead, nz - ahead) - 1, 0)
        finals.append((ahead == 0, by_cw, old[e] // nz, lane * p.steps + skew))

    cc = {}
    todo = list(range(p.steps))

    def convey(t):
        for lane in (0, 1):
            for way in (0, 1):
                n = (way * 2 + lane) * p.steps + t
                mine, ysrc, second = lanes[way, lane]
                if t > 0:
                    for inlane in (0, 1):
                        cc[way, inlane, t - 1].arrive()
                    value = jnp.where(second, cin[(way * 2 + 1) * p.steps + t - 1], cin[way * 2 * p.steps + t - 1])
                    if t < p.chunks:
                        value = jnp.where(mine, spread[ysrc, pl.ds(t * p.chunk, p.chunk)], value)
                else:
                    value = spread[ysrc, pl.ds(0, p.chunk)]
                cout[n] = value
                cc[way, lane, t] = go(cout.at[n], cin.at[n], cs.at[n], cr.at[n], along[way])

    def convey_next(count=1):
        for _ in range(count):
            if todo:
                convey(todo.pop(0))

    def choose(ny_first):
        for way in (0, 1):
            for lane in (0, 1):
                cc[way, lane, p.steps - 1].arrive()
        for j in ny_first:
            stay, by_cw, ysrc, at = finals[0]
            for yy in range(1, ny):
                here = (y + j) % ny == yy
                other = finals[yy]
                stay = (here & other[0]) | (~here & stay)
                by_cw = (here & other[1]) | (~here & by_cw)
                ysrc = jnp.where(here, other[2], ysrc)
                at = jnp.where(here, other[3], at)

            def one(k, carry):
                rows = pl.ds(pl.multiple_of(k * p.chunk, p.chunk), p.chunk)
                value = jnp.where(by_cw, cin[at + k], cin[2 * p.steps + at + k])
                fin[j, rows] = jnp.where(stay, spread[ysrc, rows], value)
                return carry

            lax.fori_loop(0, p.chunks, one, 0)

    fc = []

    def deliver():
        for j in range(1, ny):
            fc.append(go(fin.at[j], moved.at[y], fs.at[j - 1], fr.at[j - 1], above[j]))
        fc.append(local(6, fin.at[0], moved.at[y]))

    ta = lax.broadcasted_iota(jnp.int32, (tok_n, tok_n), 0)
    tb = lax.broadcasted_iota(jnp.int32, (tok_n, tok_n), 1)
    before = (ta < tb).astype(F32).astype(BF16)
    after = (tb < ta).astype(F32).astype(BF16)
    same = (ta == tb).astype(F32).astype(BF16)
    jrow = lax.broadcasted_iota(jnp.int32, (8, 1), 0)
    yrow = jnp.where(jrow + y >= ny, jrow + y - ny, jrow + y)
    column = jnp.where(jrow < ny, yrow * nz + z, -5).astype(F32)
    nt = (((1,), (1,)), ((), ()))

    def places(r):
        m = metab[r, :, pl.ds(0, tok_n)].astype(F32)
        named = jnp.zeros((8, tok_n), F32)
        ghi = jnp.zeros((8, tok_n), F32)
        glo = jnp.zeros((8, tok_n), F32)
        for k in range(4):
            hit = m[k : k + 1] == column
            named = named + jnp.where(hit, 1.0, 0.0)
            ghi = ghi + jnp.where(hit, m[4 + k : 5 + k], 0.0)
            glo = glo + jnp.where(hit, m[8 + k : 9 + k], 0.0)
        nb = named.astype(BF16)
        rank = jnp.dot(nb, before, preferred_element_type=F32)
        prow[r] = jnp.where(named > 0.5, rank, -4096.0)
        rank_c = lax.dot_general(after, nb, nt, preferred_element_type=F32)
        named_c = lax.dot_general(same, nb, nt, preferred_element_type=F32)
        gate_c = lax.dot_general(same, ghi.astype(BF16), nt, preferred_element_type=F32) + lax.dot_general(
            same, glo.astype(BF16), nt, preferred_element_type=F32
        )
        pcol[r, :, pl.ds(0, 8)] = jnp.where(named_c > 0.5, rank_c, -4096.0)
        pcol[r, :, pl.ds(8, 8)] = gate_c

    crow = lax.broadcasted_iota(jnp.int32, (p.rows, tok_n), 0).astype(F32)
    dc = {}

    def dispatch(h):
        for j in [(ny - o) % ny for o in p.yorder[1:] + p.yorder[:1]]:
            total = jnp.zeros((p.rows, p.d), F32)
            for i, r in enumerate(p.groups[h]):
                pick = jnp.where(prow[r, j : j + 1, :] + float(i * p.cap) == crow, 1.0, 0.0).astype(BF16)
                total = total + jnp.dot(pick, tokb[r], preferred_element_type=F32)
            total = total.astype(BF16)
            if j == 0:
                recvd[pl.ds(h * ny * p.rows, p.rows)] = total
            else:
                n = h * (ny - 1) + j - 1
                sendb[n] = total
                pos = p.yorder.index((ny - j) % ny)
                at = pl.ds((h * ny + pos) * p.rows, p.rows)
                dc[h, pos] = go(sendb.at[n], recvd.at[at], ds.at[n], dr.at[n], above[j])

    ec = {}

    def expert(h, first, count):
        base = (h * ny + first) * p.rows
        size = count * p.rows
        for pos in range(first, first + count):
            if pos > 0:
                dc[h, pos].arrive()

        def matrix(c, i):
            rows = pl.ds(i * p.d, p.d)
            return jnp.concatenate([wall[c, 0, rows], wall[c, 1, rows]], axis=1)

        def chunk(c, carry):
            xin = recvd[pl.ds(base, size)]
            g = jnp.dot(xin, matrix(c, 0), preferred_element_type=F32)
            u = jnp.dot(xin, matrix(c, 1), preferred_element_type=F32)
            hid = (g / (1.0 + jnp.exp(-g)) * u).astype(BF16)
            add = lax.dot_general(hid, matrix(c, 2), nt, preferred_element_type=F32)
            acc[pl.ds(0, size)] = acc[pl.ds(0, size)] + add
            return carry

        acc[pl.ds(0, size)] = jnp.zeros((size, p.d), F32)
        for part in range(0, nx, 2):
            lax.fori_loop(part, min(part + 2, nx), chunk, 0)
            convey_next()
        res[pl.ds(base, size)] = acc[pl.ds(0, size)].astype(BF16)

    def answer(h, first, count):
        for pos in range(first, first + count):
            if pos > 0:
                o = p.yorder[pos]
                j = ny - o
                n = h * (ny - 1) + j - 1
                at = pl.ds((h * ny + pos) * p.rows, p.rows)
                ec[h, j] = go(res.at[at], rret.at[n], es.at[n], er.at[n], above[o])

    ccol = lax.broadcasted_iota(jnp.int32, (tok_n, p.rows), 1).astype(F32)

    def combine(r):
        h = 0 if r in p.groups[0] else 1
        i = p.groups[h].index(r)
        total = jnp.zeros((tok_n, p.d), F32)
        for j in range(ny):
            pick = jnp.where(pcol[r, :, j : j + 1] + float(i * p.cap) == ccol, 1.0, 0.0).astype(BF16)
            rows = res[pl.ds(h * ny * p.rows, p.rows)] if j == 0 else rret[h * (ny - 1) + j - 1]
            total = total + pcol[r, :, 8 + j : 9 + j] * jnp.dot(pick, rows, preferred_element_type=F32)
        part[r] = total

    rc = {}

    def reduce_step(dist):
        for way, half, d in p.rs:
            if d == dist:
                n = p.rs.index((way, half, dist))
                first, size = p.rscut[half]
                total = part[dist if way == 0 else nz - dist, pl.ds(first, size)]
                if (way, half, dist + 1) in rc:
                    rc[way, half, dist + 1].arrive()
                    total = total + rsin[p.rs.index((way, half, dist + 1)), pl.ds(0, size)].astype(F32)
                rsout[n, pl.ds(0, size)] = total.astype(BF16)
                rows = pl.ds(0, size)
                rc[way, half, dist] = go(rsout.at[n, rows], rsin.at[n, rows], rss.at[n], rsr.at[n], along[way])

    halves = [(first, min(2, ny - first)) for first in range(0, ny, 2)]
    places(0)
    for s in range(2, p.half + 1):
        ag_step(s)
        places(s - 1)
        places(nz - s + 1)
        if s == max(2, p.half - 1):
            own_tokens.wait()
            dispatch(0)
            x_second()
    spread_ready()
    convey_next()
    for half in (0, 1, 2):
        agc[half % 2, half, p.half].arrive()
    places(p.half)
    dispatch(1)
    convey_next()
    x_third()
    x_ready()
    for h in (0, 1):
        for span in halves:
            expert(h, *span)
            if h == 1 or not FAR_FIRST:
                answer(h, *span)
    if FAR_FIRST:
        for span in halves:
            answer(0, *span)
    convey_next(len(todo))
    choose(range(ny))
    if EARLY:
        deliver()
    if not FAR_FIRST:
        for j in range(1, ny):
            ec[0, j].arrive()
        for r in p.groups[0]:
            combine(r)
    for j in range(1, ny):
        ec[1, j].arrive()
    if not EARLY and not FAR_FIRST:
        deliver()
    for dist in range(p.half, 0, -1):
        pair = sorted({dist, nz - dist})
        if FAR_FIRST and pair[0] in p.groups[0] and not fc:
            for j in range(1, ny):
                ec[0, j].arrive()
            deliver()
        elif FAR_FIRST and pair[0] in p.groups[0]:
            for j in range(1, ny):
                ec[0, j].arrive()
        for r in pair:
            if FAR_FIRST or r in p.groups[1]:
                combine(r)
        reduce_step(dist)
    if FAR_FIRST:
        combine(0)
    for half in (0, 1):
        first, size = p.rscut[half]
        total = part[0, pl.ds(first, size)]
        for way in (0, 1):
            rc[way, half, 1].arrive()
            total = total + rsin[p.rs.index((way, half, 1)), pl.ds(0, size)].astype(F32)
        out[pl.ds(first, size)] = total.astype(BF16)
    for link in started:
        link.arrive()
    fc[-1].wait()
    for link in started:
        link.copy.wait_send()


def moe(p, *operands):
    ny, nz, nx = p.ny, p.nz, p.nx
    dma = pltpu.SemaphoreType.DMA
    vmem = pl.BlockSpec(memory_space=pltpu.VMEM)
    smem = pl.BlockSpec(memory_space=pltpu.SMEM)
    anywhere = pl.BlockSpec(memory_space=pl.ANY)
    wrows = 3 * p.d
    return pl.pallas_call(
        functools.partial(moe_kernel, p),
        out_shape=(
            jax.ShapeDtypeStruct((p.tok, p.d), BF16),
            jax.ShapeDtypeStruct((ny, p.piece, p.hs), BF16),
        ),
        in_specs=[anywhere, vmem, vmem, smem, smem, anywhere, anywhere, anywhere],
        out_specs=(vmem, anywhere),
        scratch_shapes=[
            pltpu.VMEM((nz, p.tok, p.d), BF16),
            pltpu.VMEM((nz, META, -(-p.tok // 128) * 128), BF16),
            pltpu.VMEM((2 * (ny - 1), p.rows, p.d), BF16),
            pltpu.VMEM((2 * ny * p.rows, p.d), BF16),
            pltpu.VMEM((nx, 2, wrows, p.hs), BF16),
            pltpu.VMEM((2 * ny * p.rows, p.d), BF16),
            pltpu.VMEM((2 * (ny - 1), p.rows, p.d), BF16),
            pltpu.VMEM((nz, p.tok, p.d), F32),
            pltpu.VMEM((len(p.rs), p.tok // 2, p.d), BF16),
            pltpu.VMEM((len(p.rs), p.tok // 2, p.d), BF16),
            pltpu.VMEM((2 * p.rows, p.d), F32),
            pltpu.VMEM((nz, 8, p.tok), F32),
            pltpu.VMEM((nz, p.tok, 128), F32),
            pltpu.VMEM((2, wrows, p.hs), F32),
            pltpu.VMEM((3 * wrows, p.hs), BF16),
            pltpu.VMEM((ny, p.piece, p.hs), BF16),
            pltpu.VMEM((4 * p.steps, p.chunk, p.hs), BF16),
            pltpu.VMEM((4 * p.steps, p.chunk, p.hs), BF16),
            pltpu.VMEM((ny, p.piece, p.hs), BF16),
            dma((7,)),
            dma((len(p.ag),)),
            dma((len(p.ag),)),
            dma((8,)),
            dma((8,)),
            dma((2 * (ny - 1),)),
            dma((2 * (ny - 1),)),
            dma((2 * (ny - 1),)),
            dma((2 * (ny - 1),)),
            dma((len(p.rs),)),
            dma((len(p.rs),)),
            dma((ny - 1,)),
            dma((ny - 1,)),
            dma((4 * p.steps,)),
            dma((4 * p.steps,)),
            dma((ny - 1,)),
            dma((ny - 1,)),
        ],
        compiler_params=pltpu.CompilerParams(
            collective_id=0, has_side_effects=True, vmem_limit_bytes=60 * 1024 * 1024
        ),
        name="moe",
    )(*operands)


def finish_kernel(n, d, old, new, layer, wts, first_m, second_m, moved, out, w_out, f_out, s_out, lbuf, wbuf, half, full, sems):
    me = lax.axis_index("expert")
    rows = 3 * d
    cut = rows // 4

    def look(e, found):
        return jnp.where((old[e] == me) & (new[e] == me), 1, found)

    layer_in = pltpu.make_async_copy(layer, lbuf, sems.at[0])
    layer_in.start()
    stays = lax.fori_loop(0, n, look, 0) == 1

    def run(sources):
        parts = []
        for a, (src, base, mid, end, dst) in enumerate(sources):
            for i in range(4):
                at = pl.ds(i * cut, cut)
                load = pltpu.make_async_copy(src.at[pl.ds(base + i * cut, cut)], mid.at[at], sems.at[2 + a * 4 + i])
                load.start()
                parts.append((load, mid, end, dst, at, sems.at[14 + a * 4 + i]))
        stores = []
        for load, mid, end, dst, at, sem in parts:
            load.wait()
            if end is not mid:
                end[at] = mid[at].astype(F32)
            store = pltpu.make_async_copy(end.at[at], dst.at[at], sem)
            store.start()
            stores.append(store)
        for store in stores:
            store.wait()

    @pl.when(stays)
    def _():
        one, two = full.at[0], full.at[1]
        run(((wts, 0, wbuf, wbuf, w_out), (first_m, 0, one, one, f_out), (second_m, 0, two, two, s_out)))

    @pl.when(jnp.logical_not(stays))
    def _():
        run(
            (
                (moved, 0, wbuf, wbuf, w_out),
                (moved, rows, half.at[0], full.at[0], f_out),
                (moved, 2 * rows, half.at[1], full.at[1], s_out),
            )
        )

    layer_in.wait()
    layer_out = pltpu.make_async_copy(lbuf, out, sems.at[1])
    layer_out.start()
    layer_out.wait()


def finish(n, d, *operands):
    layer, wts = operands[2], operands[3]
    smem = pl.BlockSpec(memory_space=pltpu.SMEM)
    anywhere = pl.BlockSpec(memory_space=pl.ANY)
    rows, lanes = wts.shape
    return pl.pallas_call(
        functools.partial(finish_kernel, n, d),
        out_shape=(
            jax.ShapeDtypeStruct(layer.shape, layer.dtype),
            jax.ShapeDtypeStruct(wts.shape, BF16),
            jax.ShapeDtypeStruct(wts.shape, F32),
            jax.ShapeDtypeStruct(wts.shape, F32),
        ),
        in_specs=[smem, smem] + [anywhere] * 5,
        out_specs=[anywhere] * 4,
        scratch_shapes=[
            pltpu.VMEM(layer.shape, BF16),
            pltpu.VMEM((rows, lanes), BF16),
            pltpu.VMEM((2, rows, lanes), BF16),
            pltpu.VMEM((2, rows, lanes), F32),
            pltpu.SemaphoreType.DMA((26,)),
        ],
        compiler_params=pltpu.CompilerParams(vmem_limit_bytes=60 * 1024 * 1024),
        name="finish",
    )(*operands)


def per_device(n_y, tokens, route_ids, gate_weight, old_owner, new_owner, weights, first_moment, second_moment):
    n = lax.axis_size("expert")
    tok, d = tokens.shape
    hs = weights.shape[3]
    p = Plan(lax.axis_size("dp"), n_y, n // n_y, tok, 3 * tok * route_ids.shape[1] // (2 * n), d, hs)
    blocks = [a.reshape(-1, hs) for a in (weights, first_moment, second_moment)]
    layer, moved = moe(p, tokens, route_ids.T, gate_weight.T, old_owner, new_owner, *blocks)
    done = finish(n, d, old_owner, new_owner, layer, *blocks, moved.reshape(-1, hs))
    return (done[0], *(a.reshape(weights.shape) for a in done[1:]))


def solution(mesh):
    experts = mesh.shape["expert"]
    n_y = 4 if experts == 32 else 2
    placed = (
        P(("dp", "expert"), None),
        P(("dp", "expert"), None),
        P(("dp", "expert"), None),
        P(),
        P(),
        P("expert", None, None, "dp"),
        P("expert", None, None, "dp"),
        P("expert", None, None, "dp"),
    )
    return jax.shard_map(
        functools.partial(per_device, n_y),
        mesh=mesh,
        in_specs=placed,
        out_specs=(
            P(("dp", "expert"), None),
            P("expert", None, None, "dp"),
            P("expert", None, None, "dp"),
            P("expert", None, None, "dp"),
        ),
        check_vma=False,
    )
```

```python
import functools

import jax
import jax.numpy as jnp
from jax import lax
from jax.experimental import pallas as pl
from jax.experimental.pallas import tpu as pltpu
from jax.sharding import PartitionSpec as P

MESH = pl.DeviceIdType.MESH
F32 = jnp.float32
BF16 = jnp.bfloat16
META = 16
FAR_FIRST = True
EARLY = False


class Plan:
    def __init__(self, n_dp, n_y, n_z, tok, cap, d, hs):
        self.nx, self.ny, self.nz = n_dp // 2, n_y, n_z
        self.tok, self.cap, self.d, self.hs = tok, cap, d, hs
        self.half = n_z // 2
        order = [0]
        for s in range(1, self.half):
            order += [s, n_z - s]
        order += [self.half]
        self.groups = (order[: self.half], order[self.half :])
        self.rows = self.half * cap
        self.yorder = [0, 1, 3, 2] if n_y == 4 else list(range(n_y))
        self.chunks = 6
        self.steps = self.chunks + self.half - 1
        self.piece = 9 * d // n_y
        self.chunk = self.piece // self.chunks
        cut = tok // 2
        self.agcut = ((0, cut), (cut, tok - cut))
        self.rscut = ((0, cut), (cut, tok - cut))
        self.ag = [
            (way, part, s)
            for s in range(1, self.half + 1)
            for part in (0, 1, 2)
            for way in (0, 1)
            if s < self.half or way == part % 2
        ]
        self.rs = [
            (way, part, dist)
            for dist in range(self.half, 0, -1)
            for part in (0, 1)
            for way in (0, 1)
            if dist < self.half or way == part
        ]


class Link:
    def __init__(self, src, dst, send, recv, to):
        self.copy = pltpu.make_async_remote_copy(
            src_ref=src, dst_ref=dst, send_sem=send, recv_sem=recv, device_id=to, device_id_type=MESH
        )
        self.copy.start()
        self.here = False

    def arrive(self):
        if not self.here:
            self.copy.wait_recv()
            self.here = True


def moe_kernel(
    p,
    tokens,
    route,
    gate,
    old,
    new,
    wts,
    first_m,
    second_m,
    out,
    moved,
    tokb,
    metab,
    sendb,
    recvd,
    wall,
    res,
    rret,
    part,
    rsin,
    rsout,
    acc,
    prow,
    pcol,
    stage,
    block,
    spread0,
    spread1,
    cin,
    cout,
    fin,
    lsem,
    ags,
    agr,
    xs,
    xr,
    ds,
    dr,
    es,
    er,
    rss,
    rsr,
    ss,
    sr,
    cs,
    cr,
    fs,
    fr,
):
    ny, nz, nx = p.ny, p.nz, p.nx
    tok_n = p.tok
    dp = lax.axis_index("dp")
    ex = lax.axis_index("expert")
    x, core = dp // 2, dp % 2
    y, z = ex // nz, ex % nz
    right = (dp, y * nz + (z + 1) % nz)
    left = (dp, y * nz + (z + nz - 1) % nz)
    along = (right, left)
    above = [None] + [(dp, ((y + j) % ny) * nz + z) for j in range(1, ny)]
    twin = (x * 2 + 1 - core, ex)
    xright = (((x + 1) % nx) * 2 + core, ex)
    xleft = (((x + nx - 1) % nx) * 2 + core, ex)
    started = []

    def go(*what):
        link = Link(*what)
        started.append(link)
        return link

    def local(n, src, dst):
        copy = pltpu.make_async_copy(src, dst, lsem.at[n])
        copy.start()
        return copy

    own_tokens = local(0, tokens, tokb.at[0])
    own_weights = local(1, wts, wall.at[0, 0])
    wrows = 3 * p.d
    block_weights = local(2, wts, block.at[pl.ds(0, wrows)])
    stage_first = local(3, first_m, stage.at[0])
    stage_second = local(4, second_m, stage.at[1])

    barrier = pltpu.get_barrier_semaphore()
    peers = [right, left, twin] + above[1:] + ([xright, xleft] if nx > 1 else [])
    for peer in peers:
        pl.semaphore_signal(barrier, inc=1, device_id=peer, device_id_type=MESH)
    slots = jnp.zeros((4, tok_n), jnp.int32)
    for e in range(ny * nz):
        slots = jnp.where(route[...] == e, old[e], slots)
    g = gate[...]
    high = g.astype(BF16).astype(F32)
    meta = jnp.concatenate([slots.astype(F32), high, g - high, jnp.full((4, tok_n), -1.0, F32)], axis=0)
    wide = -(-tok_n // 128) * 128
    if wide > tok_n:
        meta = jnp.concatenate([meta, jnp.zeros((META, wide - tok_n), F32)], axis=1)
    metab[0] = meta.astype(BF16)
    block_weights.wait()
    stage_first.wait()
    stage_second.wait()
    step_rows = 256

    def narrow(i, carry):
        for a in (0, 1):
            rows = pl.ds(pl.multiple_of(i * step_rows, step_rows), step_rows)
            to = pl.ds(pl.multiple_of((1 + a) * wrows + i * step_rows, step_rows), step_rows)
            block[to] = stage[a, rows].astype(BF16)
        return carry

    lax.fori_loop(0, wrows // step_rows, narrow, 0)

    pl.semaphore_wait(barrier, len(peers))

    agc = {}

    def ag_send(way, half, s):
        src = (nz - (s - 1)) % nz if way == 0 else s - 1
        dst = nz - s if way == 0 else s
        n = p.ag.index((way, half, s))
        if half == 2:
            agc[way, half, s] = go(metab.at[src], metab.at[dst], ags.at[n], agr.at[n], along[way])
        else:
            rows = pl.ds(*p.agcut[half])
            source = tokens.at[rows] if s == 1 else tokb.at[src, rows]
            agc[way, half, s] = go(source, tokb.at[dst, rows], ags.at[n], agr.at[n], along[way])

    def ag_step(s):
        for way, half, step in p.ag:
            if step == s:
                agc[way, half, s - 1].arrive()
                ag_send(way, half, s)
        for way, half, step in p.ag:
            if step == s - 1:
                agc[way, half, step].arrive()

    for half in (0, 1, 2):
        for way in (0, 1):
            ag_send(way, half, 1)

    hp = p.piece // 2

    def piece(i, part):
        return block.at[pl.ds(pl.multiple_of(i * p.piece + part * hp, hp), hp)]

    spread = (spread0, spread1)
    keep_piece = [local(5 + 2 * part, piece(y, part), spread[part].at[y]) for part in (0, 1)]
    sc = ([], [])
    for cut in (0, 1):
        for j in range(1, ny):
            n = cut * (ny - 1) + j - 1
            sc[cut].append(go(piece((y + j) % ny, cut), spread[cut].at[y], ss.at[n], sr.at[n], above[j]))

    xc = [go(wts, wall.at[0, 1], xs.at[0], xr.at[0], twin)]
    if nx > 1:
        xc.append(go(wts, wall.at[3, 0], xs.at[1], xr.at[1], xright))
        xc.append(go(wts, wall.at[1, 0], xs.at[2], xr.at[2], xleft))

    def x_second():
        if nx > 1:
            lo, hi = pl.ds(0, wrows // 2), pl.ds(wrows // 2, wrows // 2)
            xc[1].arrive()
            xc.append(go(wall.at[3, 0, lo], wall.at[2, 0, lo], xs.at[3], xr.at[3], xright))
            xc.append(go(wall.at[3, 0], wall.at[3, 1], xs.at[4], xr.at[4], twin))
            xc[2].arrive()
            xc.append(go(wall.at[1, 0, hi], wall.at[2, 0, hi], xs.at[5], xr.at[5], xleft))
            xc.append(go(wall.at[1, 0], wall.at[1, 1], xs.at[6], xr.at[6], twin))

    def x_third():
        if nx > 1:
            xc[3].arrive()
            xc[5].arrive()
            xc.append(go(wall.at[2, 0], wall.at[2, 1], xs.at[7], xr.at[7], twin))

    def x_ready():
        own_weights.wait()
        for link in xc:
            link.arrive()


    def spread_ready(part):
        if not sc[part][0].here:
            keep_piece[part].wait()
        for link in sc[part]:
            link.arrive()

    def spread_rows(t):
        part = t * p.chunk // hp
        return spread[part], pl.ds(t * p.chunk - part * hp, p.chunk)

    def scan(e, carry):
        seen, named = carry
        zs, zd = old[e] % nz, new[e] % nz
        ahead = (zd - zs + nz) % nz
        seen = list(seen)
        for way in (0, 1):
            goes = (ahead >= 1) & (ahead <= p.half) if way == 0 else ahead > p.half
            far = ahead if way == 0 else nz - ahead
            for into in (0, 1):
                at = z + nz - into if way == 0 else z + into
                passed = (at - zs + nz) % nz if way == 0 else (zs - at + 2 * nz) % nz
                on = goes & (passed < far)
                n = (way * 2 + into) * 2
                seen[n] = jnp.where(on & (seen[n] < 0), e, seen[n])
                seen[n + 1] = jnp.where(on, e, seen[n + 1])
        named = tuple(jnp.where(new[e] == yy * nz + z, e, named[yy]) for yy in range(ny))
        return tuple(seen), named

    none = jnp.int32(-1)
    seen, named = lax.fori_loop(0, ny * nz, scan, ((none,) * 8, (none,) * ny))
    lanes = {}
    for way in (0, 1):
        for lane in (0, 1):
            e = jnp.maximum(seen[way * 4 + lane], 0)
            lanes[way, lane] = (old[e] % nz == z, old[e] // nz, e != seen[way * 4 + 2])
    finals = []
    for yy in range(ny):
        e = jnp.maximum(named[yy], 0)
        ahead = (new[e] % nz - old[e] % nz + nz) % nz
        by_cw = ahead <= p.half
        lane = jnp.where(e != jnp.where(by_cw, seen[2], seen[6]), 1, 0)
        skew = jnp.maximum(jnp.where(by_cw, ahead, nz - ahead) - 1, 0)
        finals.append((ahead == 0, by_cw, old[e] // nz, lane * p.steps + skew))

    cc = {}
    todo = list(range(p.steps))

    def convey(t):
        for lane in (0, 1):
            for way in (0, 1):
                n = (way * 2 + lane) * p.steps + t
                mine, ysrc, second = lanes[way, lane]
                if t < p.chunks:
                    spread_ready(t * p.chunk // hp)
                    pieces, rows = spread_rows(t)
                if t > 0:
                    for inlane in (0, 1):
                        cc[way, inlane, t - 1].arrive()
                    value = jnp.where(second, cin[(way * 2 + 1) * p.steps + t - 1], cin[way * 2 * p.steps + t - 1])
                    if t < p.chunks:
                        value = jnp.where(mine, pieces[ysrc, rows], value)
                else:
                    value = pieces[ysrc, rows]
                cout[n] = value
                cc[way, lane, t] = go(cout.at[n], cin.at[n], cs.at[n], cr.at[n], along[way])

    def convey_next(count=1):
        for _ in range(count):
            if todo:
                convey(todo.pop(0))

    def choose(ny_first):
        for way in (0, 1):
            for lane in (0, 1):
                cc[way, lane, p.steps - 1].arrive()
        for j in ny_first:
            stay, by_cw, ysrc, at = finals[0]
            for yy in range(1, ny):
                here = (y + j) % ny == yy
                other = finals[yy]
                stay = (here & other[0]) | (~here & stay)
                by_cw = (here & other[1]) | (~here & by_cw)
                ysrc = jnp.where(here, other[2], ysrc)
                at = jnp.where(here, other[3], at)

            for part in (0, 1):

                def one(k, carry):
                    rows = pl.ds(pl.multiple_of(k * p.chunk, p.chunk), p.chunk)
                    t = part * (p.chunks // 2) + k
                    value = jnp.where(by_cw, cin[at + t], cin[2 * p.steps + at + t])
                    value = jnp.where(stay, spread[part][ysrc, rows], value)
                    fin[j, pl.ds(pl.multiple_of(t * p.chunk, p.chunk), p.chunk)] = value
                    return carry

                lax.fori_loop(0, p.chunks // 2, one, 0)

    fc = []

    def deliver():
        for j in range(1, ny):
            fc.append(go(fin.at[j], moved.at[y], fs.at[j - 1], fr.at[j - 1], above[j]))
        fc.append(local(6, fin.at[0], moved.at[y]))

    ta = lax.broadcasted_iota(jnp.int32, (tok_n, tok_n), 0)
    tb = lax.broadcasted_iota(jnp.int32, (tok_n, tok_n), 1)
    before = (ta < tb).astype(F32).astype(BF16)
    after = (tb < ta).astype(F32).astype(BF16)
    same = (ta == tb).astype(F32).astype(BF16)
    jrow = lax.broadcasted_iota(jnp.int32, (8, 1), 0)
    yrow = jnp.where(jrow + y >= ny, jrow + y - ny, jrow + y)
    column = jnp.where(jrow < ny, yrow * nz + z, -5).astype(F32)
    nt = (((1,), (1,)), ((), ()))

    def places(r):
        m = metab[r, :, pl.ds(0, tok_n)].astype(F32)
        named = jnp.zeros((8, tok_n), F32)
        ghi = jnp.zeros((8, tok_n), F32)
        glo = jnp.zeros((8, tok_n), F32)
        for k in range(4):
            hit = m[k : k + 1] == column
            named = named + jnp.where(hit, 1.0, 0.0)
            ghi = ghi + jnp.where(hit, m[4 + k : 5 + k], 0.0)
            glo = glo + jnp.where(hit, m[8 + k : 9 + k], 0.0)
        nb = named.astype(BF16)
        rank = jnp.dot(nb, before, preferred_element_type=F32)
        prow[r] = jnp.where(named > 0.5, rank, -4096.0)
        rank_c = lax.dot_general(after, nb, nt, preferred_element_type=F32)
        named_c = lax.dot_general(same, nb, nt, preferred_element_type=F32)
        gate_c = lax.dot_general(same, ghi.astype(BF16), nt, preferred_element_type=F32) + lax.dot_general(
            same, glo.astype(BF16), nt, preferred_element_type=F32
        )
        pcol[r, :, pl.ds(0, 8)] = jnp.where(named_c > 0.5, rank_c, -4096.0)
        pcol[r, :, pl.ds(8, 8)] = gate_c

    crow = lax.broadcasted_iota(jnp.int32, (p.rows, tok_n), 0).astype(F32)
    dc = {}

    def dispatch(h):
        for j in [(ny - o) % ny for o in p.yorder[1:] + p.yorder[:1]]:
            total = jnp.zeros((p.rows, p.d), F32)
            for i, r in enumerate(p.groups[h]):
                pick = jnp.where(prow[r, j : j + 1, :] + float(i * p.cap) == crow, 1.0, 0.0).astype(BF16)
                total = total + jnp.dot(pick, tokb[r], preferred_element_type=F32)
            total = total.astype(BF16)
            if j == 0:
                recvd[pl.ds(h * ny * p.rows, p.rows)] = total
            else:
                n = h * (ny - 1) + j - 1
                sendb[n] = total
                pos = p.yorder.index((ny - j) % ny)
                at = pl.ds((h * ny + pos) * p.rows, p.rows)
                dc[h, pos] = go(sendb.at[n], recvd.at[at], ds.at[n], dr.at[n], above[j])

    ec = {}

    def expert(h, first, count):
        base = (h * ny + first) * p.rows
        size = count * p.rows
        for pos in range(first, first + count):
            if pos > 0:
                dc[h, pos].arrive()

        def matrix(c, i):
            rows = pl.ds(i * p.d, p.d)
            return jnp.concatenate([wall[c, 0, rows], wall[c, 1, rows]], axis=1)

        def chunk(c, carry):
            xin = recvd[pl.ds(base, size)]
            g = jnp.dot(xin, matrix(c, 0), preferred_element_type=F32)
            u = jnp.dot(xin, matrix(c, 1), preferred_element_type=F32)
            hid = (g / (1.0 + jnp.exp(-g)) * u).astype(BF16)
            add = lax.dot_general(hid, matrix(c, 2), nt, preferred_element_type=F32)
            acc[pl.ds(0, size)] = acc[pl.ds(0, size)] + add
            return carry

        acc[pl.ds(0, size)] = jnp.zeros((size, p.d), F32)
        for part in range(0, nx, 2):
            lax.fori_loop(part, min(part + 2, nx), chunk, 0)
            if part == 0:
                convey_next()
        res[pl.ds(base, size)] = acc[pl.ds(0, size)].astype(BF16)

    def answer(h, first, count):
        for pos in range(first, first + count):
            if pos > 0:
                o = p.yorder[pos]
                j = ny - o
                n = h * (ny - 1) + j - 1
                at = pl.ds((h * ny + pos) * p.rows, p.rows)
                ec[h, j] = go(res.at[at], rret.at[n], es.at[n], er.at[n], above[o])

    ccol = lax.broadcasted_iota(jnp.int32, (tok_n, p.rows), 1).astype(F32)

    def combine(r):
        h = 0 if r in p.groups[0] else 1
        i = p.groups[h].index(r)
        total = jnp.zeros((tok_n, p.d), F32)
        for j in range(ny):
            pick = jnp.where(pcol[r, :, j : j + 1] + float(i * p.cap) == ccol, 1.0, 0.0).astype(BF16)
            rows = res[pl.ds(h * ny * p.rows, p.rows)] if j == 0 else rret[h * (ny - 1) + j - 1]
            total = total + pcol[r, :, 8 + j : 9 + j] * jnp.dot(pick, rows, preferred_element_type=F32)
        part[r] = total

    rc = {}

    def reduce_step(dist):
        for way, half, d in p.rs:
            if d == dist:
                n = p.rs.index((way, half, dist))
                first, size = p.rscut[half]
                total = part[dist if way == 0 else nz - dist, pl.ds(first, size)]
                if (way, half, dist + 1) in rc:
                    rc[way, half, dist + 1].arrive()
                    total = total + rsin[p.rs.index((way, half, dist + 1)), pl.ds(0, size)].astype(F32)
                rsout[n, pl.ds(0, size)] = total.astype(BF16)
                rows = pl.ds(0, size)
                rc[way, half, dist] = go(rsout.at[n, rows], rsin.at[n, rows], rss.at[n], rsr.at[n], along[way])

    halves = [(first, min(2, ny - first)) for first in range(0, ny, 2)]
    places(0)
    for s in range(2, p.half + 1):
        ag_step(s)
        places(s - 1)
        places(nz - s + 1)
        if s == max(2, p.half - 1):
            own_tokens.wait()
            dispatch(0)
            x_second()
            convey_next()
    convey_next()
    for half in (0, 1, 2):
        agc[half % 2, half, p.half].arrive()
    places(p.half)
    dispatch(1)
    convey_next()
    x_third()
    x_ready()
    for h in (0, 1):
        for span in halves:
            expert(h, *span)
            if h == 1 or not FAR_FIRST:
                answer(h, *span)
    if FAR_FIRST:
        for span in halves:
            answer(0, *span)
    convey_next(len(todo))
    choose(range(ny))
    if EARLY:
        deliver()
    if not FAR_FIRST:
        for j in range(1, ny):
            ec[0, j].arrive()
        for r in p.groups[0]:
            combine(r)
    for j in range(1, ny):
        ec[1, j].arrive()
    if not EARLY and not FAR_FIRST:
        deliver()
    for dist in range(p.half, 0, -1):
        pair = sorted({dist, nz - dist})
        if FAR_FIRST and pair[0] in p.groups[0] and not fc:
            for j in range(1, ny):
                ec[0, j].arrive()
            deliver()
        elif FAR_FIRST and pair[0] in p.groups[0]:
            for j in range(1, ny):
                ec[0, j].arrive()
        for r in pair:
            if FAR_FIRST or r in p.groups[1]:
                combine(r)
        reduce_step(dist)
    if FAR_FIRST:
        combine(0)
    for half in (0, 1):
        first, size = p.rscut[half]
        total = part[0, pl.ds(first, size)]
        for way in (0, 1):
            rc[way, half, 1].arrive()
            total = total + rsin[p.rs.index((way, half, 1)), pl.ds(0, size)].astype(F32)
        out[pl.ds(first, size)] = total.astype(BF16)
    for link in started:
        link.arrive()
    fc[-1].wait()
    for link in started:
        link.copy.wait_send()


def moe(p, *operands):
    ny, nz, nx = p.ny, p.nz, p.nx
    dma = pltpu.SemaphoreType.DMA
    vmem = pl.BlockSpec(memory_space=pltpu.VMEM)
    smem = pl.BlockSpec(memory_space=pltpu.SMEM)
    anywhere = pl.BlockSpec(memory_space=pl.ANY)
    wrows = 3 * p.d
    return pl.pallas_call(
        functools.partial(moe_kernel, p),
        out_shape=(
            jax.ShapeDtypeStruct((p.tok, p.d), BF16),
            jax.ShapeDtypeStruct((ny, p.piece, p.hs), BF16),
        ),
        in_specs=[anywhere, vmem, vmem, smem, smem, anywhere, anywhere, anywhere],
        out_specs=(vmem, anywhere),
        scratch_shapes=[
            pltpu.VMEM((nz, p.tok, p.d), BF16),
            pltpu.VMEM((nz, META, -(-p.tok // 128) * 128), BF16),
            pltpu.VMEM((2 * (ny - 1), p.rows, p.d), BF16),
            pltpu.VMEM((2 * ny * p.rows, p.d), BF16),
            pltpu.VMEM((nx, 2, wrows, p.hs), BF16),
            pltpu.VMEM((2 * ny * p.rows, p.d), BF16),
            pltpu.VMEM((2 * (ny - 1), p.rows, p.d), BF16),
            pltpu.VMEM((nz, p.tok, p.d), F32),
            pltpu.VMEM((len(p.rs), p.tok // 2, p.d), BF16),
            pltpu.VMEM((len(p.rs), p.tok // 2, p.d), BF16),
            pltpu.VMEM((2 * p.rows, p.d), F32),
            pltpu.VMEM((nz, 8, p.tok), F32),
            pltpu.VMEM((nz, p.tok, 128), F32),
            pltpu.VMEM((2, wrows, p.hs), F32),
            pltpu.VMEM((3 * wrows, p.hs), BF16),
            pltpu.VMEM((ny, p.piece // 2, p.hs), BF16),
            pltpu.VMEM((ny, p.piece // 2, p.hs), BF16),
            pltpu.VMEM((4 * p.steps, p.chunk, p.hs), BF16),
            pltpu.VMEM((4 * p.steps, p.chunk, p.hs), BF16),
            pltpu.VMEM((ny, p.piece, p.hs), BF16),
            dma((8,)),
            dma((len(p.ag),)),
            dma((len(p.ag),)),
            dma((8,)),
            dma((8,)),
            dma((2 * (ny - 1),)),
            dma((2 * (ny - 1),)),
            dma((2 * (ny - 1),)),
            dma((2 * (ny - 1),)),
            dma((len(p.rs),)),
            dma((len(p.rs),)),
            dma((2 * (ny - 1),)),
            dma((2 * (ny - 1),)),
            dma((4 * p.steps,)),
            dma((4 * p.steps,)),
            dma((ny - 1,)),
            dma((ny - 1,)),
        ],
        compiler_params=pltpu.CompilerParams(
            collective_id=0, has_side_effects=True, vmem_limit_bytes=60 * 1024 * 1024
        ),
        name="moe",
    )(*operands)


def finish_kernel(n, d, old, new, layer, wts, first_m, second_m, moved, out, w_out, f_out, s_out, lbuf, wbuf, half, full, sems):
    me = lax.axis_index("expert")
    rows = 3 * d
    cut = rows // 4

    def look(e, found):
        return jnp.where((old[e] == me) & (new[e] == me), 1, found)

    layer_in = pltpu.make_async_copy(layer, lbuf, sems.at[0])
    layer_in.start()
    stays = lax.fori_loop(0, n, look, 0) == 1

    def run(sources):
        parts = []
        for a, (src, base, mid, end, dst) in enumerate(sources):
            for i in range(4):
                at = pl.ds(i * cut, cut)
                load = pltpu.make_async_copy(src.at[pl.ds(base + i * cut, cut)], mid.at[at], sems.at[2 + a * 4 + i])
                load.start()
                parts.append((load, mid, end, dst, at, sems.at[14 + a * 4 + i]))
        stores = []
        for load, mid, end, dst, at, sem in parts:
            load.wait()
            if end is not mid:
                end[at] = mid[at].astype(F32)
            store = pltpu.make_async_copy(end.at[at], dst.at[at], sem)
            store.start()
            stores.append(store)
        for store in stores:
            store.wait()

    @pl.when(stays)
    def _():
        one, two = full.at[0], full.at[1]
        run(((wts, 0, wbuf, wbuf, w_out), (first_m, 0, one, one, f_out), (second_m, 0, two, two, s_out)))

    @pl.when(jnp.logical_not(stays))
    def _():
        run(
            (
                (moved, 0, wbuf, wbuf, w_out),
                (moved, rows, half.at[0], full.at[0], f_out),
                (moved, 2 * rows, half.at[1], full.at[1], s_out),
            )
        )

    layer_in.wait()
    layer_out = pltpu.make_async_copy(lbuf, out, sems.at[1])
    layer_out.start()
    layer_out.wait()


def finish(n, d, *operands):
    layer, wts = operands[2], operands[3]
    smem = pl.BlockSpec(memory_space=pltpu.SMEM)
    anywhere = pl.BlockSpec(memory_space=pl.ANY)
    rows, lanes = wts.shape
    return pl.pallas_call(
        functools.partial(finish_kernel, n, d),
        out_shape=(
            jax.ShapeDtypeStruct(layer.shape, layer.dtype),
            jax.ShapeDtypeStruct(wts.shape, BF16),
            jax.ShapeDtypeStruct(wts.shape, F32),
            jax.ShapeDtypeStruct(wts.shape, F32),
        ),
        in_specs=[smem, smem] + [anywhere] * 5,
        out_specs=[anywhere] * 4,
        scratch_shapes=[
            pltpu.VMEM(layer.shape, BF16),
            pltpu.VMEM((rows, lanes), BF16),
            pltpu.VMEM((2, rows, lanes), BF16),
            pltpu.VMEM((2, rows, lanes), F32),
            pltpu.SemaphoreType.DMA((26,)),
        ],
        compiler_params=pltpu.CompilerParams(vmem_limit_bytes=60 * 1024 * 1024),
        name="finish",
    )(*operands)


def per_device(n_y, tokens, route_ids, gate_weight, old_owner, new_owner, weights, first_moment, second_moment):
    n = lax.axis_size("expert")
    tok, d = tokens.shape
    hs = weights.shape[3]
    p = Plan(lax.axis_size("dp"), n_y, n // n_y, tok, 3 * tok * route_ids.shape[1] // (2 * n), d, hs)
    blocks = [a.reshape(-1, hs) for a in (weights, first_moment, second_moment)]
    layer, moved = moe(p, tokens, route_ids.T, gate_weight.T, old_owner, new_owner, *blocks)
    done = finish(n, d, old_owner, new_owner, layer, *blocks, moved.reshape(-1, hs))
    return (done[0], *(a.reshape(weights.shape) for a in done[1:]))


def solution(mesh):
    experts = mesh.shape["expert"]
    n_y = 4 if experts == 32 else 2
    placed = (
        P(("dp", "expert"), None),
        P(("dp", "expert"), None),
        P(("dp", "expert"), None),
        P(),
        P(),
        P("expert", None, None, "dp"),
        P("expert", None, None, "dp"),
        P("expert", None, None, "dp"),
    )
    return jax.shard_map(
        functools.partial(per_device, n_y),
        mesh=mesh,
        in_specs=placed,
        out_specs=(
            P(("dp", "expert"), None),
            P("expert", None, None, "dp"),
            P("expert", None, None, "dp"),
            P("expert", None, None, "dp"),
        ),
        check_vma=False,
    )
```

```python
import functools

import jax
import jax.numpy as jnp
from jax import lax
from jax.experimental import pallas as pl
from jax.experimental.pallas import tpu as pltpu
from jax.sharding import PartitionSpec as P

MESH = pl.DeviceIdType.MESH
F32 = jnp.float32
BF16 = jnp.bfloat16
META = 16
FAR_FIRST = True
EARLY = False


class Plan:
    def __init__(self, n_dp, n_y, n_z, tok, cap, d, hs):
        self.nx, self.ny, self.nz = n_dp // 2, n_y, n_z
        self.tok, self.cap, self.d, self.hs = tok, cap, d, hs
        self.half = n_z // 2
        order = [0]
        for s in range(1, self.half):
            order += [s, n_z - s]
        order += [self.half]
        self.groups = (order[: self.half], order[self.half :])
        self.rows = self.half * cap
        self.yorder = [0, 1, 3, 2] if n_y == 4 else list(range(n_y))
        self.chunks = 4
        self.steps = self.chunks + self.half - 1
        self.piece = 9 * d // n_y
        self.chunk = self.piece // self.chunks
        cut = tok // 2
        self.agcut = ((0, cut), (cut, tok - cut))
        self.rscut = ((0, cut), (cut, tok - cut))
        self.ag = [
            (way, part, s)
            for s in range(1, self.half + 1)
            for part in (0, 1, 2)
            for way in (0, 1)
            if s < self.half or way == part % 2
        ]
        self.rs = [
            (way, part, dist)
            for dist in range(self.half, 0, -1)
            for part in (0, 1)
            for way in (0, 1)
            if dist < self.half or way == part
        ]


class Link:
    def __init__(self, src, dst, send, recv, to):
        self.copy = pltpu.make_async_remote_copy(
            src_ref=src, dst_ref=dst, send_sem=send, recv_sem=recv, device_id=to, device_id_type=MESH
        )
        self.copy.start()
        self.here = False

    def arrive(self):
        if not self.here:
            self.copy.wait_recv()
            self.here = True


def moe_kernel(
    p,
    tokens,
    route,
    gate,
    old,
    new,
    wts,
    first_m,
    second_m,
    out,
    moved,
    tokb,
    metab,
    sendb,
    recvd,
    wall,
    res,
    rret,
    part,
    rsin,
    rsout,
    acc,
    prow,
    pcol,
    stage,
    block,
    spread0,
    spread1,
    cin,
    cout,
    fin,
    lsem,
    ags,
    agr,
    xs,
    xr,
    ds,
    dr,
    es,
    er,
    rss,
    rsr,
    ss,
    sr,
    cs,
    cr,
    fs,
    fr,
):
    ny, nz, nx = p.ny, p.nz, p.nx
    tok_n = p.tok
    dp = lax.axis_index("dp")
    ex = lax.axis_index("expert")
    x, core = dp // 2, dp % 2
    y, z = ex // nz, ex % nz
    right = (dp, y * nz + (z + 1) % nz)
    left = (dp, y * nz + (z + nz - 1) % nz)
    along = (right, left)
    above = [None] + [(dp, ((y + j) % ny) * nz + z) for j in range(1, ny)]
    twin = (x * 2 + 1 - core, ex)
    xright = (((x + 1) % nx) * 2 + core, ex)
    xleft = (((x + nx - 1) % nx) * 2 + core, ex)
    started = []

    def go(*what):
        link = Link(*what)
        started.append(link)
        return link

    def local(n, src, dst):
        copy = pltpu.make_async_copy(src, dst, lsem.at[n])
        copy.start()
        return copy

    own_tokens = local(0, tokens, tokb.at[0])
    own_weights = local(1, wts, wall.at[0, 0])
    wrows = 3 * p.d
    block_weights = local(2, wts, block.at[pl.ds(0, wrows)])
    stage_first = local(3, first_m, stage.at[0])
    stage_second = local(4, second_m, stage.at[1])

    barrier = pltpu.get_barrier_semaphore()
    peers = [right, left, twin] + above[1:] + ([xright, xleft] if nx > 1 else [])
    for peer in peers:
        pl.semaphore_signal(barrier, inc=1, device_id=peer, device_id_type=MESH)
    slots = jnp.zeros((4, tok_n), jnp.int32)
    for e in range(ny * nz):
        slots = jnp.where(route[...] == e, old[e], slots)
    g = gate[...]
    high = g.astype(BF16).astype(F32)
    meta = jnp.concatenate([slots.astype(F32), high, g - high, jnp.full((4, tok_n), -1.0, F32)], axis=0)
    wide = -(-tok_n // 128) * 128
    if wide > tok_n:
        meta = jnp.concatenate([meta, jnp.zeros((META, wide - tok_n), F32)], axis=1)
    metab[0] = meta.astype(BF16)
    block_weights.wait()
    stage_first.wait()
    stage_second.wait()
    step_rows = 256

    def narrow(i, carry):
        for a in (0, 1):
            rows = pl.ds(pl.multiple_of(i * step_rows, step_rows), step_rows)
            to = pl.ds(pl.multiple_of((1 + a) * wrows + i * step_rows, step_rows), step_rows)
            block[to] = stage[a, rows].astype(BF16)
        return carry

    lax.fori_loop(0, wrows // step_rows, narrow, 0)

    pl.semaphore_wait(barrier, len(peers))

    agc = {}

    def ag_send(way, half, s):
        src = (nz - (s - 1)) % nz if way == 0 else s - 1
        dst = nz - s if way == 0 else s
        n = p.ag.index((way, half, s))
        if half == 2:
            agc[way, half, s] = go(metab.at[src], metab.at[dst], ags.at[n], agr.at[n], along[way])
        else:
            rows = pl.ds(*p.agcut[half])
            source = tokens.at[rows] if s == 1 else tokb.at[src, rows]
            agc[way, half, s] = go(source, tokb.at[dst, rows], ags.at[n], agr.at[n], along[way])

    def ag_step(s):
        for way, half, step in p.ag:
            if step == s:
                agc[way, half, s - 1].arrive()
                ag_send(way, half, s)
        for way, half, step in p.ag:
            if step == s - 1:
                agc[way, half, step].arrive()

    for half in (0, 1, 2):
        for way in (0, 1):
            ag_send(way, half, 1)

    hp = p.piece // 2

    def piece(i, part):
        return block.at[pl.ds(pl.multiple_of(i * p.piece + part * hp, hp), hp)]

    spread = (spread0, spread1)
    keep_piece = [local(5 + 2 * part, piece(y, part), spread[part].at[y]) for part in (0, 1)]
    sc = ([], [])
    for cut in (0, 1):
        for j in range(1, ny):
            n = cut * (ny - 1) + j - 1
            sc[cut].append(go(piece((y + j) % ny, cut), spread[cut].at[y], ss.at[n], sr.at[n], above[j]))

    xc = [go(wts, wall.at[0, 1], xs.at[0], xr.at[0], twin)]
    if nx > 1:
        xc.append(go(wts, wall.at[3, 0], xs.at[1], xr.at[1], xright))
        xc.append(go(wts, wall.at[1, 0], xs.at[2], xr.at[2], xleft))

    def x_second():
        if nx > 1:
            lo, hi = pl.ds(0, wrows // 2), pl.ds(wrows // 2, wrows // 2)
            xc[1].arrive()
            xc.append(go(wall.at[3, 0, lo], wall.at[2, 0, lo], xs.at[3], xr.at[3], xright))
            xc.append(go(wall.at[3, 0], wall.at[3, 1], xs.at[4], xr.at[4], twin))
            xc[2].arrive()
            xc.append(go(wall.at[1, 0, hi], wall.at[2, 0, hi], xs.at[5], xr.at[5], xleft))
            xc.append(go(wall.at[1, 0], wall.at[1, 1], xs.at[6], xr.at[6], twin))

    def x_third():
        if nx > 1:
            xc[3].arrive()
            xc[5].arrive()
            xc.append(go(wall.at[2, 0], wall.at[2, 1], xs.at[7], xr.at[7], twin))

    def x_ready():
        own_weights.wait()
        for link in xc:
            link.arrive()


    def spread_ready(part):
        if not sc[part][0].here:
            keep_piece[part].wait()
        for link in sc[part]:
            link.arrive()

    def spread_rows(t):
        part = t * p.chunk // hp
        return spread[part], pl.ds(t * p.chunk - part * hp, p.chunk)

    def scan(e, carry):
        seen, named = carry
        zs, zd = old[e] % nz, new[e] % nz
        ahead = (zd - zs + nz) % nz
        seen = list(seen)
        for way in (0, 1):
            goes = (ahead >= 1) & (ahead <= p.half) if way == 0 else ahead > p.half
            far = ahead if way == 0 else nz - ahead
            for into in (0, 1):
                at = z + nz - into if way == 0 else z + into
                passed = (at - zs + nz) % nz if way == 0 else (zs - at + 2 * nz) % nz
                on = goes & (passed < far)
                n = (way * 2 + into) * 2
                seen[n] = jnp.where(on & (seen[n] < 0), e, seen[n])
                seen[n + 1] = jnp.where(on, e, seen[n + 1])
        named = tuple(jnp.where(new[e] == yy * nz + z, e, named[yy]) for yy in range(ny))
        return tuple(seen), named

    none = jnp.int32(-1)
    seen, named = lax.fori_loop(0, ny * nz, scan, ((none,) * 8, (none,) * ny))
    lanes = {}
    for way in (0, 1):
        for lane in (0, 1):
            e = jnp.maximum(seen[way * 4 + lane], 0)
            lanes[way, lane] = (old[e] % nz == z, old[e] // nz, e != seen[way * 4 + 2])
    finals = []
    for yy in range(ny):
        e = jnp.maximum(named[yy], 0)
        ahead = (new[e] % nz - old[e] % nz + nz) % nz
        by_cw = ahead <= p.half
        lane = jnp.where(e != jnp.where(by_cw, seen[2], seen[6]), 1, 0)
        skew = jnp.maximum(jnp.where(by_cw, ahead, nz - ahead) - 1, 0)
        finals.append((ahead == 0, by_cw, old[e] // nz, lane * p.steps + skew))

    cc = {}
    todo = list(range(p.steps))

    def convey(t):
        for lane in (0, 1):
            for way in (0, 1):
                n = (way * 2 + lane) * p.steps + t
                mine, ysrc, second = lanes[way, lane]
                if t < p.chunks:
                    spread_ready(t * p.chunk // hp)
                    pieces, rows = spread_rows(t)
                if t > 0:
                    for inlane in (0, 1):
                        cc[way, inlane, t - 1].arrive()
                    value = jnp.where(second, cin[(way * 2 + 1) * p.steps + t - 1], cin[way * 2 * p.steps + t - 1])
                    if t < p.chunks:
                        value = jnp.where(mine, pieces[ysrc, rows], value)
                else:
                    value = pieces[ysrc, rows]
                cout[n] = value
                cc[way, lane, t] = go(cout.at[n], cin.at[n], cs.at[n], cr.at[n], along[way])

    def convey_next(count=1):
        for _ in range(count):
            if todo:
                convey(todo.pop(0))

    def choose(ny_first):
        for way in (0, 1):
            for lane in (0, 1):
                cc[way, lane, p.steps - 1].arrive()
        for j in ny_first:
            stay, by_cw, ysrc, at = finals[0]
            for yy in range(1, ny):
                here = (y + j) % ny == yy
                other = finals[yy]
                stay = (here & other[0]) | (~here & stay)
                by_cw = (here & other[1]) | (~here & by_cw)
                ysrc = jnp.where(here, other[2], ysrc)
                at = jnp.where(here, other[3], at)

            for part in (0, 1):

                def one(k, carry):
                    rows = pl.ds(pl.multiple_of(k * p.chunk, p.chunk), p.chunk)
                    t = part * (p.chunks // 2) + k
                    value = jnp.where(by_cw, cin[at + t], cin[2 * p.steps + at + t])
                    value = jnp.where(stay, spread[part][ysrc, rows], value)
                    fin[j, pl.ds(pl.multiple_of(t * p.chunk, p.chunk), p.chunk)] = value
                    return carry

                lax.fori_loop(0, p.chunks // 2, one, 0)

    fc = []

    def deliver():
        for j in range(1, ny):
            fc.append(go(fin.at[j], moved.at[y], fs.at[j - 1], fr.at[j - 1], above[j]))
        fc.append(local(6, fin.at[0], moved.at[y]))

    ta = lax.broadcasted_iota(jnp.int32, (tok_n, tok_n), 0)
    tb = lax.broadcasted_iota(jnp.int32, (tok_n, tok_n), 1)
    before = (ta < tb).astype(F32).astype(BF16)
    after = (tb < ta).astype(F32).astype(BF16)
    same = (ta == tb).astype(F32).astype(BF16)
    jrow = lax.broadcasted_iota(jnp.int32, (8, 1), 0)
    yrow = jnp.where(jrow + y >= ny, jrow + y - ny, jrow + y)
    column = jnp.where(jrow < ny, yrow * nz + z, -5).astype(F32)
    nt = (((1,), (1,)), ((), ()))

    def places(r):
        m = metab[r, :, pl.ds(0, tok_n)].astype(F32)
        named = jnp.zeros((8, tok_n), F32)
        ghi = jnp.zeros((8, tok_n), F32)
        glo = jnp.zeros((8, tok_n), F32)
        for k in range(4):
            hit = m[k : k + 1] == column
            named = named + jnp.where(hit, 1.0, 0.0)
            ghi = ghi + jnp.where(hit, m[4 + k : 5 + k], 0.0)
            glo = glo + jnp.where(hit, m[8 + k : 9 + k], 0.0)
        nb = named.astype(BF16)
        rank = jnp.dot(nb, before, preferred_element_type=F32)
        prow[r] = jnp.where(named > 0.5, rank, -4096.0)
        rank_c = lax.dot_general(after, nb, nt, preferred_element_type=F32)
        named_c = lax.dot_general(same, nb, nt, preferred_element_type=F32)
        gate_c = lax.dot_general(same, ghi.astype(BF16), nt, preferred_element_type=F32) + lax.dot_general(
            same, glo.astype(BF16), nt, preferred_element_type=F32
        )
        pcol[r, :, pl.ds(0, 8)] = jnp.where(named_c > 0.5, rank_c, -4096.0)
        pcol[r, :, pl.ds(8, 8)] = gate_c

    crow = lax.broadcasted_iota(jnp.int32, (p.rows, tok_n), 0).astype(F32)
    dc = {}

    def dispatch(h):
        for j in [(ny - o) % ny for o in p.yorder[1:] + p.yorder[:1]]:
            total = jnp.zeros((p.rows, p.d), F32)
            for i, r in enumerate(p.groups[h]):
                pick = jnp.where(prow[r, j : j + 1, :] + float(i * p.cap) == crow, 1.0, 0.0).astype(BF16)
                total = total + jnp.dot(pick, tokb[r], preferred_element_type=F32)
            total = total.astype(BF16)
            if j == 0:
                recvd[pl.ds(h * ny * p.rows, p.rows)] = total
            else:
                n = h * (ny - 1) + j - 1
                sendb[n] = total
                pos = p.yorder.index((ny - j) % ny)
                at = pl.ds((h * ny + pos) * p.rows, p.rows)
                dc[h, pos] = go(sendb.at[n], recvd.at[at], ds.at[n], dr.at[n], above[j])

    ec = {}

    def expert(h, first, count):
        base = (h * ny + first) * p.rows
        size = count * p.rows
        for pos in range(first, first + count):
            if pos > 0:
                dc[h, pos].arrive()

        def matrix(c, i):
            rows = pl.ds(i * p.d, p.d)
            return jnp.concatenate([wall[c, 0, rows], wall[c, 1, rows]], axis=1)

        def chunk(c, carry):
            xin = recvd[pl.ds(base, size)]
            g = jnp.dot(xin, matrix(c, 0), preferred_element_type=F32)
            u = jnp.dot(xin, matrix(c, 1), preferred_element_type=F32)
            hid = (g / (1.0 + jnp.exp(-g)) * u).astype(BF16)
            add = lax.dot_general(hid, matrix(c, 2), nt, preferred_element_type=F32)
            acc[pl.ds(0, size)] = acc[pl.ds(0, size)] + add
            return carry

        acc[pl.ds(0, size)] = jnp.zeros((size, p.d), F32)
        for part in range(0, nx, 2):
            lax.fori_loop(part, min(part + 2, nx), chunk, 0)
            if part == 0:
                convey_next()
        res[pl.ds(base, size)] = acc[pl.ds(0, size)].astype(BF16)

    def answer(h, first, count):
        for pos in range(first, first + count):
            if pos > 0:
                o = p.yorder[pos]
                j = ny - o
                n = h * (ny - 1) + j - 1
                at = pl.ds((h * ny + pos) * p.rows, p.rows)
                ec[h, j] = go(res.at[at], rret.at[n], es.at[n], er.at[n], above[o])

    ccol = lax.broadcasted_iota(jnp.int32, (tok_n, p.rows), 1).astype(F32)

    def combine(r):
        h = 0 if r in p.groups[0] else 1
        i = p.groups[h].index(r)
        total = jnp.zeros((tok_n, p.d), F32)
        for j in range(ny):
            pick = jnp.where(pcol[r, :, j : j + 1] + float(i * p.cap) == ccol, 1.0, 0.0).astype(BF16)
            rows = res[pl.ds(h * ny * p.rows, p.rows)] if j == 0 else rret[h * (ny - 1) + j - 1]
            total = total + pcol[r, :, 8 + j : 9 + j] * jnp.dot(pick, rows, preferred_element_type=F32)
        part[r] = total

    rc = {}

    def reduce_step(dist):
        for way, half, d in p.rs:
            if d == dist:
                n = p.rs.index((way, half, dist))
                first, size = p.rscut[half]
                total = part[dist if way == 0 else nz - dist, pl.ds(first, size)]
                if (way, half, dist + 1) in rc:
                    rc[way, half, dist + 1].arrive()
                    total = total + rsin[p.rs.index((way, half, dist + 1)), pl.ds(0, size)].astype(F32)
                rsout[n, pl.ds(0, size)] = total.astype(BF16)
                rows = pl.ds(0, size)
                rc[way, half, dist] = go(rsout.at[n, rows], rsin.at[n, rows], rss.at[n], rsr.at[n], along[way])

    halves = [(first, min(2, ny - first)) for first in range(0, ny, 2)]
    places(0)
    for s in range(2, p.half + 1):
        ag_step(s)
        places(s - 1)
        places(nz - s + 1)
        if s == max(2, p.half - 1):
            own_tokens.wait()
            dispatch(0)
            x_second()
            convey_next()
    convey_next()
    for half in (0, 1, 2):
        agc[half % 2, half, p.half].arrive()
    places(p.half)
    dispatch(1)
    convey_next()
    x_third()
    x_ready()
    for h in (0, 1):
        for span in halves:
            expert(h, *span)
            if h == 1 or not FAR_FIRST:
                answer(h, *span)
    if FAR_FIRST:
        for span in halves:
            answer(0, *span)
    convey_next(len(todo))
    choose(range(ny))
    if EARLY:
        deliver()
    if not FAR_FIRST:
        for j in range(1, ny):
            ec[0, j].arrive()
        for r in p.groups[0]:
            combine(r)
    for j in range(1, ny):
        ec[1, j].arrive()
    if not EARLY and not FAR_FIRST:
        deliver()
    for dist in range(p.half, 0, -1):
        pair = sorted({dist, nz - dist})
        if FAR_FIRST and pair[0] in p.groups[0] and not fc:
            for j in range(1, ny):
                ec[0, j].arrive()
            deliver()
        elif FAR_FIRST and pair[0] in p.groups[0]:
            for j in range(1, ny):
                ec[0, j].arrive()
        for r in pair:
            if FAR_FIRST or r in p.groups[1]:
                combine(r)
        reduce_step(dist)
    if FAR_FIRST:
        combine(0)
    for half in (0, 1):
        first, size = p.rscut[half]
        total = part[0, pl.ds(first, size)]
        for way in (0, 1):
            rc[way, half, 1].arrive()
            total = total + rsin[p.rs.index((way, half, 1)), pl.ds(0, size)].astype(F32)
        out[pl.ds(first, size)] = total.astype(BF16)
    for link in started:
        link.arrive()
    fc[-1].wait()
    for link in started:
        link.copy.wait_send()


def moe(p, *operands):
    ny, nz, nx = p.ny, p.nz, p.nx
    dma = pltpu.SemaphoreType.DMA
    vmem = pl.BlockSpec(memory_space=pltpu.VMEM)
    smem = pl.BlockSpec(memory_space=pltpu.SMEM)
    anywhere = pl.BlockSpec(memory_space=pl.ANY)
    wrows = 3 * p.d
    return pl.pallas_call(
        functools.partial(moe_kernel, p),
        out_shape=(
            jax.ShapeDtypeStruct((p.tok, p.d), BF16),
            jax.ShapeDtypeStruct((ny, p.piece, p.hs), BF16),
        ),
        in_specs=[anywhere, vmem, vmem, smem, smem, anywhere, anywhere, anywhere],
        out_specs=(vmem, anywhere),
        scratch_shapes=[
            pltpu.VMEM((nz, p.tok, p.d), BF16),
            pltpu.VMEM((nz, META, -(-p.tok // 128) * 128), BF16),
            pltpu.VMEM((2 * (ny - 1), p.rows, p.d), BF16),
            pltpu.VMEM((2 * ny * p.rows, p.d), BF16),
            pltpu.VMEM((nx, 2, wrows, p.hs), BF16),
            pltpu.VMEM((2 * ny * p.rows, p.d), BF16),
            pltpu.VMEM((2 * (ny - 1), p.rows, p.d), BF16),
            pltpu.VMEM((nz, p.tok, p.d), F32),
            pltpu.VMEM((len(p.rs), p.tok // 2, p.d), BF16),
            pltpu.VMEM((len(p.rs), p.tok // 2, p.d), BF16),
            pltpu.VMEM((2 * p.rows, p.d), F32),
            pltpu.VMEM((nz, 8, p.tok), F32),
            pltpu.VMEM((nz, p.tok, 128), F32),
            pltpu.VMEM((2, wrows, p.hs), F32),
            pltpu.VMEM((3 * wrows, p.hs), BF16),
            pltpu.VMEM((ny, p.piece // 2, p.hs), BF16),
            pltpu.VMEM((ny, p.piece // 2, p.hs), BF16),
            pltpu.VMEM((4 * p.steps, p.chunk, p.hs), BF16),
            pltpu.VMEM((4 * p.steps, p.chunk, p.hs), BF16),
            pltpu.VMEM((ny, p.piece, p.hs), BF16),
            dma((8,)),
            dma((len(p.ag),)),
            dma((len(p.ag),)),
            dma((8,)),
            dma((8,)),
            dma((2 * (ny - 1),)),
            dma((2 * (ny - 1),)),
            dma((2 * (ny - 1),)),
            dma((2 * (ny - 1),)),
            dma((len(p.rs),)),
            dma((len(p.rs),)),
            dma((2 * (ny - 1),)),
            dma((2 * (ny - 1),)),
            dma((4 * p.steps,)),
            dma((4 * p.steps,)),
            dma((ny - 1,)),
            dma((ny - 1,)),
        ],
        compiler_params=pltpu.CompilerParams(
            collective_id=0, has_side_effects=True, vmem_limit_bytes=60 * 1024 * 1024
        ),
        name="moe",
    )(*operands)


def finish_kernel(n, d, old, new, layer, wts, first_m, second_m, moved, out, w_out, f_out, s_out, lbuf, wbuf, half, full, sems):
    me = lax.axis_index("expert")
    rows = 3 * d
    cut = rows // 4

    def look(e, found):
        return jnp.where((old[e] == me) & (new[e] == me), 1, found)

    layer_in = pltpu.make_async_copy(layer, lbuf, sems.at[0])
    layer_in.start()
    stays = lax.fori_loop(0, n, look, 0) == 1

    def run(sources):
        parts = []
        for a, (src, base, mid, end, dst) in enumerate(sources):
            for i in range(4):
                at = pl.ds(i * cut, cut)
                load = pltpu.make_async_copy(src.at[pl.ds(base + i * cut, cut)], mid.at[at], sems.at[2 + a * 4 + i])
                load.start()
                parts.append((load, mid, end, dst, at, sems.at[14 + a * 4 + i]))
        stores = []
        for load, mid, end, dst, at, sem in parts:
            load.wait()
            if end is not mid:
                end[at] = mid[at].astype(F32)
            store = pltpu.make_async_copy(end.at[at], dst.at[at], sem)
            store.start()
            stores.append(store)
        for store in stores:
            store.wait()

    @pl.when(stays)
    def _():
        one, two = full.at[0], full.at[1]
        run(((wts, 0, wbuf, wbuf, w_out), (first_m, 0, one, one, f_out), (second_m, 0, two, two, s_out)))

    @pl.when(jnp.logical_not(stays))
    def _():
        run(
            (
                (moved, 0, wbuf, wbuf, w_out),
                (moved, rows, half.at[0], full.at[0], f_out),
                (moved, 2 * rows, half.at[1], full.at[1], s_out),
            )
        )

    layer_in.wait()
    layer_out = pltpu.make_async_copy(lbuf, out, sems.at[1])
    layer_out.start()
    layer_out.wait()


def finish(n, d, *operands):
    layer, wts = operands[2], operands[3]
    smem = pl.BlockSpec(memory_space=pltpu.SMEM)
    anywhere = pl.BlockSpec(memory_space=pl.ANY)
    rows, lanes = wts.shape
    return pl.pallas_call(
        functools.partial(finish_kernel, n, d),
        out_shape=(
            jax.ShapeDtypeStruct(layer.shape, layer.dtype),
            jax.ShapeDtypeStruct(wts.shape, BF16),
            jax.ShapeDtypeStruct(wts.shape, F32),
            jax.ShapeDtypeStruct(wts.shape, F32),
        ),
        in_specs=[smem, smem] + [anywhere] * 5,
        out_specs=[anywhere] * 4,
        scratch_shapes=[
            pltpu.VMEM(layer.shape, BF16),
            pltpu.VMEM((rows, lanes), BF16),
            pltpu.VMEM((2, rows, lanes), BF16),
            pltpu.VMEM((2, rows, lanes), F32),
            pltpu.SemaphoreType.DMA((26,)),
        ],
        compiler_params=pltpu.CompilerParams(vmem_limit_bytes=60 * 1024 * 1024),
        name="finish",
    )(*operands)


def per_device(n_y, tokens, route_ids, gate_weight, old_owner, new_owner, weights, first_moment, second_moment):
    n = lax.axis_size("expert")
    tok, d = tokens.shape
    hs = weights.shape[3]
    p = Plan(lax.axis_size("dp"), n_y, n // n_y, tok, 3 * tok * route_ids.shape[1] // (2 * n), d, hs)
    blocks = [a.reshape(-1, hs) for a in (weights, first_moment, second_moment)]
    layer, moved = moe(p, tokens, route_ids.T, gate_weight.T, old_owner, new_owner, *blocks)
    done = finish(n, d, old_owner, new_owner, layer, *blocks, moved.reshape(-1, hs))
    return (done[0], *(a.reshape(weights.shape) for a in done[1:]))


def solution(mesh):
    experts = mesh.shape["expert"]
    n_y = 4 if experts == 32 else 2
    placed = (
        P(("dp", "expert"), None),
        P(("dp", "expert"), None),
        P(("dp", "expert"), None),
        P(),
        P(),
        P("expert", None, None, "dp"),
        P("expert", None, None, "dp"),
        P("expert", None, None, "dp"),
    )
    return jax.shard_map(
        functools.partial(per_device, n_y),
        mesh=mesh,
        in_specs=placed,
        out_specs=(
            P(("dp", "expert"), None),
            P("expert", None, None, "dp"),
            P("expert", None, None, "dp"),
            P("expert", None, None, "dp"),
        ),
        check_vma=False,
    )
```
